256 devices in a mesh: dp: 32 (over x, y, z_lo), tensor: 8 (over z_hi, core).
Axes of the slice: x: 4, y: 4, z: 8 (z_hi: 4, z_lo: 2; z = z_hi * 2 + z_lo), core: 2. Of those that a mesh axis runs over, the one named last changes fastest.
Arguments:
- residual: bfloat16 [32768, 4096], P(('dp', 'tensor')), parts along dimension 0, may hold values from -6 to 6
- norm_gain: float32 [4096], replicated, may hold values from 0.5 to 2
- doc_ids: int32 [32768], P('dp'), parts along dimension 0, may hold values from 0 to 3, never falling along the last dimension, each value on 1 to 512 neighbouring positions
- w_query: bfloat16 [4096, 4096], P(None, 'tensor'), as said below
- w_key: bfloat16 [4096, 1024], P(None, 'tensor'), as said below
- w_value: bfloat16 [4096, 1024], P(None, 'tensor'), may hold values from -0.09375 to 0.09375
- w_out: bfloat16 [4096, 4096], P('tensor'), may hold values from -0.25 to 0.25
Outputs:
- updated: bfloat16 [32768, 4096], P(('dp', 'tensor')), parts along dimension 0
The draws below stay inside these ranges and needn't reach their ends.
There are 32 independent parts, one for each index of `dp`. The reference program is written for one: setup_inputs(seed, part) draws one part's arguments, and reference() takes and returns one part's arrays. A program takes and returns all parts, laid end to end along the dimension named above; an argument that names none is the same for every part. Nothing has to cross between parts.
Inputs may be any that keep to these rules, and one draw needn't show every extreme that they name: `doc_ids`: document numbers never fall; every document has 1 to 512 tokens and one has exactly 512. `w_query`: entries of order 4096^-0.5. `w_key`: entries of order 4096^-0.5 or larger.
All inputs are finite; a program needn't handle non-finite values.
Results may differ from the reference program's by a relative error of at most 0.012.
The reference program's roundings to bfloat16 on the way count: a program that leaves them out, or rounds other values in their place, can miss the bound.
Values may be sent and summed in bfloat16 or wider, within the bound.
No kernel may reach another device: no remote copies, remote signals or barrier semaphores. Data moves between devices by JAX's collectives and lax.ppermute only.
A program may use at most 128 MiB of HBM per device.

```python
import math
import jax
import jax.numpy as jnp
import numpy as np
from jax import lax

D = 4096
HD = 128
HEADS_DEV = 4
HEADS = 32
KV_HEADS = 8
TOKENS = 1024
N_TENSOR = 8


def query_base(key):
    return jax.random.normal(jax.random.fold_in(key, 17), (D, HEADS * HD), jnp.float32) / math.sqrt(D)


def draw_w_query(key, part):
    return query_base(key).astype(jnp.bfloat16)


def draw_w_key(key, part):
    key = jax.random.fold_in(key, 3)
    fresh = jax.random.normal(key, (D, KV_HEADS * HD), jnp.float32) / math.sqrt(D)
    return fresh.astype(jnp.bfloat16)


def level_of(key, extent, cuts, least, largest):
    gain, own = 1.0, jax.random.fold_in(key, 6)
    for axis_at, shards_of in cuts:
        heights = jnp.exp(jax.random.uniform(jax.random.fold_in(own, axis_at), (shards_of,), jnp.float32, least / len(cuts), largest / len(cuts)))
        gain = gain * jnp.repeat(heights, extent[axis_at] // shards_of).reshape([-1 if axis == axis_at else 1 for axis in range(len(extent))])
    return gain


def split_up(number_of, total, limit, slope):
    weights = [(1 << 20) // math.isqrt(grade ** slope) + 1 for grade in range(2, number_of + 1)]
    spare, given = total - limit - (number_of - 1), [1] * (number_of - 1)
    while spare > 0:
        candidates = [i for i in range(number_of - 1) if given[i] < limit]
        pool, remaining = sum([weights[i] for i in candidates]), spare
        for i in candidates:
            extra = min(limit - given[i], max(1, remaining * weights[i] // pool), spare)
            given[i] = given[i] + extra
            spare = spare - extra
    return np.array([limit] + given)


def ragged_sizes(rng, count, total, most, lean):
    if count == 2:
        one = jax.random.randint(rng, (), max(1, total - most), min(most, total - 1) + 1)
        return jnp.stack([one, total - one])
    tallies = jnp.asarray(split_up(count, total, most, lean), jnp.int32)
    couples = (count - 1) // 2
    giver, sink = tallies[1:1 + 2 * couples:2], tallies[2:2 + 2 * couples:2]
    slack = jnp.minimum(giver - 1, most - sink)
    shifted = jax.random.randint(jax.random.fold_in(rng, 1), (couples,), 0, 1 << 20) % (slack + 1)
    tallies = tallies.at[1:1 + 2 * couples:2].set(giver - shifted).at[2:2 + 2 * couples:2].set(sink + shifted)
    return tallies[jax.random.permutation(jax.random.fold_in(rng, 2), count)]


def centred(key, extent, spread, bound, pieces=(), held_as=jnp.bfloat16):
    values = jax.random.normal(key, extent, jnp.float32) * spread
    if len(pieces) > 0:
        values = level_of(key, extent, pieces, -0.22, 0.18) * values
    return jnp.clip(values, min=-bound, max=bound).astype(held_as)


def setup_inputs(seed: int = 0, part: int = 0) -> dict:
    key_of = jax.random.split(jax.random.key(seed), 8)
    part_splits = jax.random.split(jax.random.fold_in(key_of[7], part), 8)
    residual = centred(part_splits[0], (TOKENS, D), 1.0, 6.0, ((0, 8),))
    norm_gain = jnp.clip(jnp.exp(jax.random.uniform(key_of[1], (D,), jnp.float32, math.log(0.5), math.log(2.0))), 0.5, 2.0)
    doc_ids = jnp.searchsorted(jnp.cumsum(ragged_sizes(part_splits[2], 4, TOKENS, TOKENS // 2, 0)), jnp.arange(TOKENS), side="right").astype(jnp.int32)
    w_query = draw_w_query(jax.random.fold_in(key_of[7], 71), part)
    w_key = draw_w_key(jax.random.fold_in(key_of[7], 71), part)
    w_value = centred(key_of[5], (D, KV_HEADS * HD), D ** -0.5, 0.09375, ((1, 8),))
    w_out = centred(key_of[6], (HEADS * HD, D), (D // 9) ** -0.5, 0.25, ((0, 8),))
    return dict(residual=residual, norm_gain=norm_gain, doc_ids=doc_ids, w_query=w_query, w_key=w_key, w_value=w_value, w_out=w_out)


ROPE_BASE = 500000.0

def rms_norm(rows, norm_gain):
    wide = rows.astype(jnp.float32)
    scale = lax.rsqrt(lax.optimization_barrier(jnp.mean(wide * wide, axis=-1, keepdims=True)) + 1e-05)
    return (wide * scale * norm_gain).astype(jnp.bfloat16)

def positions_of(doc_ids):
    length = doc_ids.shape[0]
    index = jnp.arange(length, dtype=jnp.int32)
    earlier = jnp.concatenate([doc_ids[:1] - 1, doc_ids[:-1]])
    starts = lax.cummax(jnp.where(doc_ids != earlier, index, jnp.zeros_like(index)), axis=0)
    return (index - starts, index)

def rotate(values, positions):
    half = values.shape[-1] // 2
    freq = ROPE_BASE ** (-jnp.arange(half, dtype=jnp.float32) / half)
    angle = positions.astype(jnp.float32)[:, None] * freq[None, :]
    cosine = jnp.cos(angle)[:, None, :]
    sine = jnp.sin(angle)[:, None, :]
    first = values[..., :half]
    second = values[..., half:]
    return jnp.concatenate([first * cosine - second * sine, second * cosine + first * sine], axis=-1)

def attend(query, key_head, value_head, allowed):
    scores = jnp.einsum('tgd,sd->gts', query.astype(jnp.float32), key_head.astype(jnp.float32))
    scores = scores / jnp.sqrt(jnp.float32(query.shape[-1]))
    scores = jnp.where(allowed[None], scores, jnp.float32(-1e+30))
    top = lax.optimization_barrier(jnp.max(scores, axis=-1, keepdims=True))
    expo = jnp.exp(scores - top)
    weights = (expo / lax.optimization_barrier(jnp.sum(expo, axis=-1, keepdims=True))).astype(jnp.bfloat16)
    context = jnp.einsum('gts,sd->tgd', weights.astype(jnp.float32), value_head.astype(jnp.float32))
    return context.astype(jnp.bfloat16).reshape(query.shape[0], query.shape[1] * query.shape[2])

def reference(residual, norm_gain, doc_ids, w_query, w_key, w_value, w_out):
    length = residual.shape[0]
    normed = rms_norm(residual, norm_gain)
    positions, index = positions_of(doc_ids)
    allowed = (doc_ids[:, None] == doc_ids[None, :]) & (index[None, :] <= index[:, None])
    query = jnp.dot(normed, w_query, preferred_element_type=jnp.float32).reshape(length, HEADS, HD)
    query = rotate(query, positions).astype(jnp.bfloat16)
    keys = jnp.dot(normed, w_key, preferred_element_type=jnp.float32).reshape(length, KV_HEADS, HD)
    keys = rotate(keys, positions).astype(jnp.bfloat16)
    values = jnp.dot(normed, w_value, preferred_element_type=jnp.float32).astype(jnp.bfloat16)
    values = values.reshape(length, KV_HEADS, HD)
    total = jnp.zeros((length, D), jnp.float32)
    width = HEADS_DEV * HD
    for group in range(N_TENSOR):
        context = attend(query[:, group * HEADS_DEV:(group + 1) * HEADS_DEV], keys[:, group], values[:, group], allowed)
        partial_value = jnp.dot(context, w_out[group * width:(group + 1) * width], preferred_element_type=jnp.float32)
        total = total + lax.optimization_barrier(partial_value.astype(jnp.bfloat16)).astype(jnp.float32)
    return (residual.astype(jnp.float32) + total).astype(jnp.bfloat16)
```

```python
import functools
import math

import jax
import jax.numpy as jnp
from jax import lax
from jax.experimental import pallas as pl
from jax.experimental.pallas import tpu as pltpu
from jax.sharding import Mesh, PartitionSpec as P

HD = 128
ROPE_BASE = 500000.0
MIB = 1024 * 1024
F32 = jnp.float32
BF16 = jnp.bfloat16
ALL = ("x", "y", "zl", "zh", "c")


def params(mib):
    return pltpu.CompilerParams(vmem_limit_bytes=mib * MIB)


def cost(flops, bytes_accessed, transcendentals=0):
    return pl.CostEstimate(
        flops=int(flops), bytes_accessed=int(bytes_accessed), transcendentals=int(transcendentals)
    )


def norm_kernel(rows_ref, gain_ref, first_ref, second_ref):
    half = first_ref.shape[0]
    for at, out_ref in ((0, first_ref), (half, second_ref)):
        wide = rows_ref[at : at + half, :].astype(F32)
        scale = lax.rsqrt(jnp.mean(wide * wide, axis=-1, keepdims=True) + 1e-05)
        out_ref[...] = (wide * scale * gain_ref[...]).astype(BF16)


def norm(residual, gain):
    rows, width = residual.shape
    half = jax.ShapeDtypeStruct((rows // 2, width), BF16)
    return pl.pallas_call(
        norm_kernel,
        out_shape=(half, half),
        compiler_params=params(58),
        cost_estimate=cost(4 * rows * width, 4 * rows * width),
        name="norm",
    )(residual, gain.reshape(1, width))


def qkv_kernel(p0, p1, p2, p3, wq, wk, wv, table_ref, out_ref, lhs, weights, lhs_sem, sems):
    rows, depth = lhs.shape
    width = wq.shape[1]
    piece = rows // 4
    chunks = sems.shape[0]
    step = depth // chunks
    copies = []
    for at, part in enumerate((p0, p1, p2, p3)):
        copies.append(
            pltpu.make_async_copy(part, lhs.at[pl.ds(at * piece, piece), :], lhs_sem.at[at])
        )
        copies[-1].start()
    loads = []
    for chunk in range(chunks):
        span = pl.ds(chunk * step, step)
        group = [
            pltpu.make_async_copy(
                wq.at[span, :], weights.at[span, pl.ds(0, width)], sems.at[chunk, 0]
            ),
            pltpu.make_async_copy(
                wk.at[span, :], weights.at[span, pl.ds(width, HD)], sems.at[chunk, 1]
            ),
            pltpu.make_async_copy(
                wv.at[span, :], weights.at[span, pl.ds(width + HD, HD)], sems.at[chunk, 2]
            ),
        ]
        for copy in group:
            copy.start()
        loads.append(group)
    for copy in copies:
        copy.wait()
    acc = None
    for chunk in range(chunks):
        for copy in loads[chunk]:
            copy.wait()
        product = jnp.dot(
            lhs[:, chunk * step : (chunk + 1) * step],
            weights[chunk * step : (chunk + 1) * step, :],
            preferred_element_type=F32,
        )
        acc = product if acc is None else acc + product
    cosine, sine = table_ref[:, :HD], table_ref[:, HD : 2 * HD]
    for at in range(0, width + HD, HD):
        part = acc[:, at : at + HD]
        turned = part * cosine + pltpu.roll(part, HD // 2, 1) * sine
        out_ref[:, at : at + HD] = turned.astype(BF16)
    out_ref[:, width + HD :] = acc[:, width + HD :].astype(BF16)


def project(pieces, wq, wk, wv, table, at):
    piece_rows, depth = pieces[0].shape
    rows = piece_rows * 4
    width = wq.shape[1] + 2 * HD
    chunks = 4
    anywhere = pl.BlockSpec(memory_space=pl.ANY)
    return pl.pallas_call(
        qkv_kernel,
        grid=(1,),
        in_specs=[anywhere] * 7 + [pl.BlockSpec((None, rows, 3 * HD), lambda k: (at, 0, 0))],
        out_specs=pl.BlockSpec((rows, width), lambda k: (0, 0)),
        out_shape=jax.ShapeDtypeStruct((rows, width), BF16),
        scratch_shapes=[
            pltpu.VMEM((rows, depth), BF16),
            pltpu.VMEM((depth, width), BF16),
            pltpu.SemaphoreType.DMA((4,)),
            pltpu.SemaphoreType.DMA((chunks, 3)),
        ],
        compiler_params=params(58),
        cost_estimate=cost(2 * rows * depth * width, 2 * depth * (rows + width)),
        name="project",
    )(*pieces, wq, wk, wv, table)


def attend_kernel(at, place, q_ref, kv0, kv1, kv2, start_ref, out_ref):
    rows = q_ref.shape[0]
    chip, core = place[0], place[1]

    def index(block, axis):
        local = lax.broadcasted_iota(jnp.int32, (rows, rows), axis)
        local = lax.rem(local + core * (rows // 2), rows)
        return lax.rem(chip + (block % 4), 4) * rows + local

    query_at = index(at, 0)
    start = start_ref[:, :1].astype(jnp.int32)
    bias = []
    for block in (at, at - 1, at - 2):
        key_at = index(block, 1)
        allowed = (key_at <= query_at) & (key_at >= start)
        bias.append(jnp.where(allowed, F32(0.0), F32(-1e30)))
    bias = jnp.concatenate(bias, axis=1)
    keys = jnp.concatenate([kv0[:, :HD], kv1[:, :HD], kv2[:, :HD]], axis=0)
    values = jnp.concatenate([kv0[:, HD:], kv1[:, HD:], kv2[:, HD:]], axis=0)
    for head in range(0, q_ref.shape[1], HD):
        scores = lax.dot_general(
            q_ref[:, head : head + HD],
            keys,
            (((1,), (1,)), ((), ())),
            preferred_element_type=F32,
        )
        scores = scores * F32(1.0 / math.sqrt(HD)) + bias
        top = jnp.max(scores, axis=-1, keepdims=True)
        expo = jnp.exp(scores - top)
        total = jnp.sum(expo, axis=-1, keepdims=True)
        context = jnp.dot(expo.astype(BF16), values, preferred_element_type=F32)
        out_ref[:, head : head + HD] = (context / total).astype(BF16)


def attend(at, place, blocks, table):
    rows = blocks[0].shape[0]
    width = blocks[0].shape[1] - 2 * HD
    query = pl.BlockSpec((rows, width), lambda h, place: (0, 0))
    pair = pl.BlockSpec((rows, 2 * HD), lambda h, place: (0, width // (2 * HD)))
    return pl.pallas_call(
        functools.partial(attend_kernel, at),
        grid_spec=pltpu.PrefetchScalarGridSpec(
            num_scalar_prefetch=1,
            grid=(1,),
            in_specs=[query]
            + [pair] * 3
            + [pl.BlockSpec((None, rows, HD), lambda h, place: (at, 0, 2))],
            out_specs=query,
        ),
        out_shape=jax.ShapeDtypeStruct((rows, width), BF16),
        compiler_params=params(58),
        cost_estimate=cost(12 * rows * rows * width, 8 * rows * width, 12 * rows * rows),
        name="attend",
    )(place, blocks[0], blocks[0], blocks[1], blocks[2], table)


def near_kernel(own, other, near_own, near_other, total_ref):
    half = own.shape[0] // 2
    first = jnp.dot(own[...], near_own[...], preferred_element_type=F32)
    turned = jnp.concatenate([other[half:, :], other[:half, :]], axis=0)
    total_ref[...] = first + jnp.dot(turned, near_other[...], preferred_element_type=F32)


def project_near(own, other, near_own, near_other):
    rows, depth = own.shape
    width, tile = near_own.shape[1], 512
    whole = pl.BlockSpec((rows, depth), lambda n: (0, 0))
    near = pl.BlockSpec((depth, tile), lambda n: (0, n))
    return pl.pallas_call(
        near_kernel,
        grid=(width // tile,),
        in_specs=[whole] * 2 + [near] * 2,
        out_specs=pl.BlockSpec((rows, tile), lambda n: (0, n)),
        out_shape=jax.ShapeDtypeStruct((rows, width), F32),
        compiler_params=params(58),
        cost_estimate=cost(4 * rows * depth * width, 4 * depth * width),
        name="project_near",
    )(own, other, near_own, near_other)


def out_kernel(o0, o1, o2, t0, t1, t2, far, total_ref, res_own, res_other, out_own, out_other, lhs):
    half = res_own.shape[0]
    depth = o0.shape[1]

    @pl.when(pl.program_id(0) == 0)
    def _():
        for r, (own, other) in enumerate(((o0, t0), (o1, t1), (o2, t2))):
            at = 2 * r * depth
            lhs[:, at : at + depth] = own[...]
            lhs[:half, at + depth : at + 2 * depth] = other[half:, :]
            lhs[half:, at + depth : at + 2 * depth] = other[:half, :]

    piece = far.shape[-1]
    rhs = jnp.concatenate(
        [far[p].reshape(lhs.shape[1], piece) for p in range(far.shape[0])], axis=1
    )
    total = total_ref[...] + jnp.dot(lhs[...], rhs, preferred_element_type=F32)
    out_own[...] = (res_own[...].astype(F32) + total[:half]).astype(BF16)
    out_other[...] = (res_other[...].astype(F32) + total[half:]).astype(BF16)


def project_out(own, other, far, total, res_own, res_other):
    rows, depth = own[0].shape
    half, width = res_own.shape
    tile = 256
    whole = pl.BlockSpec((rows, depth), lambda n: (0, 0))
    piece = far.shape[-1]
    away = pl.BlockSpec((tile // piece, 3, 2, depth, piece), lambda n: (n, 0, 0, 0, 0))
    flat = pl.BlockSpec((half, tile), lambda n: (0, n))
    out = jax.ShapeDtypeStruct((half, width), BF16)
    return pl.pallas_call(
        out_kernel,
        grid=(width // tile,),
        in_specs=[whole] * 6 + [away, pl.BlockSpec((rows, tile), lambda n: (0, n))] + [flat] * 2,
        out_specs=[flat, flat],
        out_shape=[out, out],
        scratch_shapes=[pltpu.VMEM((rows, 6 * depth), BF16)],
        compiler_params=params(58),
        cost_estimate=cost(2 * rows * 6 * depth * width, 12 * depth * width),
        name="project_out",
    )(*own, *other, far, total, res_own, res_other)


def join_kernel(place, own_ref, back_ref, out_ref):
    @pl.when(pl.program_id(0) == 0)
    def _():
        out_ref[...] = own_ref[...]

    @pl.when(pl.program_id(0) == 1)
    def _():
        out_ref[...] = back_ref[...]


def join(place, own, back):
    rows, width = own.shape
    whole = pl.BlockSpec((rows, width), lambda n, place: (0, 0))
    return pl.pallas_call(
        join_kernel,
        grid_spec=pltpu.PrefetchScalarGridSpec(
            num_scalar_prefetch=1,
            grid=(2,),
            in_specs=[whole, whole],
            out_specs=pl.BlockSpec(
                (rows, width), lambda n, place: (0, lax.rem(place[1] + n, 2))
            ),
        ),
        out_shape=jax.ShapeDtypeStruct((rows, 2 * width), BF16),
        compiler_params=params(58),
        cost_estimate=cost(0, 8 * rows * width),
        name="join",
    )(place, own, back)


def local(residual, norm_gain, doc_ids, w_query, w_key, w_value, w_out):
    length = doc_ids.shape[0]
    rows, features = residual.shape
    n_z, chip_rows = 4, 2 * rows
    zh, core = lax.axis_index("zh"), lax.axis_index("c")
    column = lax.axis_index("x") * 4 + lax.axis_index("y")
    half = features // 2
    piece = half // 16

    def move(value, by, swap=0):
        perm = [
            (2 * z + c, 2 * ((z + by) % n_z) + (c ^ swap)) for z in range(n_z) for c in range(2)
        ]
        return lax.ppermute(value, ("zh", "c"), perm)

    def swap(value):
        return move(value, 0, 1)

    keep = lax.dynamic_slice_in_dim(w_out, core * half + column * piece, piece, 1)
    give = lax.dynamic_slice_in_dim(w_out, (1 - core) * half + column * piece, piece, 1)
    near = jnp.stack([keep, swap(give)])
    first, second = norm(residual, norm_gain)
    near, first, second = lax.optimization_barrier((near, first, second))
    far = lax.all_gather(jnp.stack([move(near, -r) for r in (1, 2, 3)]), ("x", "y"), axis=0)

    def relative(values):
        turned = lax.dynamic_slice_in_dim(
            jnp.concatenate([values, values]), zh * chip_rows, length, 0
        ).reshape(n_z, 2, rows)
        return jnp.where(core == 0, turned, turned[:, ::-1]).reshape(n_z, chip_rows)

    documents = relative(doc_ids)
    start = jnp.sum((doc_ids < documents[:, :, None]).astype(jnp.int32), axis=-1)
    chips = (zh + jnp.arange(n_z, dtype=jnp.int32)) % n_z
    cores = core ^ jnp.arange(2, dtype=jnp.int32)
    at = (2 * chips[:, None] + cores)[:, :, None] * rows + jnp.arange(rows, dtype=jnp.int32)
    at = at.reshape(n_z, chip_rows)
    freq = ROPE_BASE ** (-jnp.arange(HD // 2, dtype=F32) / (HD // 2))
    angle = (at - start).astype(F32)[:, :, None] * freq
    cosine, sine = jnp.cos(angle), jnp.sin(angle)
    wide = jnp.broadcast_to(start.astype(F32)[:, :, None], (n_z, chip_rows, HD))
    table = jnp.concatenate([cosine, cosine, -sine, sine, wide], axis=-1)
    place = jnp.concatenate([zh[None], core[None]])

    def heads(r, a, b):
        return project((a, b, swap(a), swap(b)), w_query, w_key, w_value, table, r)

    qkv = [None] * 4
    up_first, down_second = move(first, 1), move(second, -1)
    up_second, down_first = move(second, 1), move(first, -1)
    qkv[0] = heads(0, first, second)
    up_first, down_second, qkv[0] = lax.optimization_barrier((up_first, down_second, qkv[0]))
    far_first, far_second = move(up_first, 1), move(down_second, -1)
    qkv[3] = heads(3, up_first, up_second)
    qkv[1] = heads(1, down_first, down_second)
    far_first, far_second, qkv[3], qkv[1] = lax.optimization_barrier(
        (far_first, far_second, qkv[3], qkv[1])
    )
    qkv[2] = heads(2, far_first, far_second)

    own, other = [None] * 4, [None] * 4
    for r in (1, 2, 3, 0):
        context = attend(r, place, [qkv[r], qkv[(r - 1) % 4], qkv[(r - 2) % 4]], table)
        source = -r % 4
        own[source] = move(context, r) if r else context
        other[source] = swap(own[source])

    near_own = lax.dynamic_slice_in_dim(w_out, core * half, half, 1)
    near_other = swap(lax.dynamic_slice_in_dim(w_out, (1 - core) * half, half, 1))
    res_own = lax.dynamic_slice_in_dim(residual, core * half, half, 1)
    res_other = swap(lax.dynamic_slice_in_dim(residual, (1 - core) * half, half, 1))
    total = project_near(own[0], other[0], near_own, near_other)
    out_own, out_other = project_out(own[1:], other[1:], far, total, res_own, res_other)
    return join(place, out_own, swap(out_other))


def solution(mesh):
    fine = Mesh(mesh.devices.reshape(4, 4, 2, 4, 2), ALL)
    seq, tensor = ("x", "y", "zl"), ("zh", "c")
    placed = (
        P(ALL, None),
        P(),
        P(seq),
        P(None, tensor),
        P(None, tensor),
        P(None, tensor),
        P(tensor, None),
    )
    return jax.shard_map(local, mesh=fine, in_specs=placed, out_specs=P(ALL, None), check_vma=False)
```

```python
import functools
import math

import jax
import jax.numpy as jnp
from jax import lax
from jax.experimental import pallas as pl
from jax.experimental.pallas import tpu as pltpu
from jax.sharding import Mesh, PartitionSpec as P

HD = 128
ROPE_BASE = 500000.0
MIB = 1024 * 1024
F32 = jnp.float32
BF16 = jnp.bfloat16
ALL = ("x", "y", "zl", "zh", "c")


def params(mib):
    return pltpu.CompilerParams(vmem_limit_bytes=mib * MIB)


def cost(flops, bytes_accessed, transcendentals=0):
    return pl.CostEstimate(
        flops=int(flops), bytes_accessed=int(bytes_accessed), transcendentals=int(transcendentals)
    )


def norm_kernel(rows_ref, gain_ref, first_ref, second_ref):
    half = first_ref.shape[0]
    for at, out_ref in ((0, first_ref), (half, second_ref)):
        wide = rows_ref[at : at + half, :].astype(F32)
        scale = lax.rsqrt(jnp.mean(wide * wide, axis=-1, keepdims=True) + 1e-05)
        out_ref[...] = (wide * scale * gain_ref[...]).astype(BF16)


def norm(residual, gain):
    rows, width = residual.shape
    half = jax.ShapeDtypeStruct((rows // 2, width), BF16)
    return pl.pallas_call(
        norm_kernel,
        out_shape=(half, half),
        compiler_params=params(58),
        cost_estimate=cost(4 * rows * width, 4 * rows * width),
        name="norm",
    )(residual, gain.reshape(1, width))


def qkv_kernel(count, *refs):
    pieces, (wq, wk, wv) = refs[:count], refs[count : count + 3]
    groups = count // 4
    tables = refs[count + 3 : count + 3 + groups]
    outs = refs[count + 3 + groups : count + 3 + 2 * groups]
    lhs, weights, lhs_sem, sems = refs[count + 3 + 2 * groups :]
    piece = pieces[0].shape[0]
    rows = 4 * piece
    width = wq.shape[1]
    pair = 2 * HD
    first = [
        pltpu.make_async_copy(part, lhs.at[pl.ds(at * piece, piece), :], lhs_sem.at[at])
        for at, part in enumerate(pieces)
    ]
    loads = [
        [
            pltpu.make_async_copy(wk, weights.at[0, :, pl.ds(0, HD)], sems.at[0]),
            pltpu.make_async_copy(wv, weights.at[0, :, pl.ds(HD, HD)], sems.at[1]),
        ]
    ]
    for at in range(width // pair):
        part = wq.at[:, pl.ds(at * pair, pair)]
        loads.append([pltpu.make_async_copy(part, weights.at[at + 1], sems.at[at + 2])])
    for copy in first + loads[0] + loads[1]:
        copy.start()
    for copy in first:
        copy.wait()
    for step, group in enumerate(loads):
        for copy in group:
            copy.wait()
        if step and step + 1 < len(loads):
            for copy in loads[step + 1]:
                copy.start()
        for block in range(groups):
            table, out_ref = tables[block], outs[block]
            cosine, sine = table[:, :HD], table[:, HD : 2 * HD]

            def turn(part):
                return (part * cosine + pltpu.roll(part, HD // 2, 1) * sine).astype(BF16)

            product = jnp.dot(
                lhs[block * rows : (block + 1) * rows, :],
                weights[step],
                preferred_element_type=F32,
            )
            if step == 0:
                out_ref[:, width : width + HD] = turn(product[:, :HD])
                out_ref[:, width + HD :] = product[:, HD:].astype(BF16)
            else:
                at = (step - 1) * pair
                out_ref[:, at : at + HD] = turn(product[:, :HD])
                out_ref[:, at + HD : at + pair] = turn(product[:, HD:])


def project(pieces, wq, wk, wv, table, blocks):
    piece_rows, depth = pieces[0].shape
    count, groups = len(pieces), len(blocks)
    rows = piece_rows * 4
    width = wq.shape[1] + 2 * HD
    steps = width // (2 * HD)
    anywhere = pl.BlockSpec(memory_space=pl.ANY)

    def angles(at):
        return pl.BlockSpec((None, rows, 2 * HD), lambda k: (at, 0, 0))

    out = jax.ShapeDtypeStruct((rows, width), BF16)
    return pl.pallas_call(
        functools.partial(qkv_kernel, count),
        grid=(1,),
        in_specs=[anywhere] * (count + 3) + [angles(at) for at in blocks],
        out_specs=[pl.BlockSpec((rows, width), lambda k: (0, 0))] * groups,
        out_shape=[out] * groups,
        scratch_shapes=[
            pltpu.VMEM((rows * groups, depth), BF16),
            pltpu.VMEM((steps, depth, 2 * HD), BF16),
            pltpu.SemaphoreType.DMA((count,)),
            pltpu.SemaphoreType.DMA((steps + 1,)),
        ],
        compiler_params=params(58),
        cost_estimate=cost(2 * rows * groups * depth * width, 2 * depth * (rows * groups + width)),
        name="project",
    )(*pieces, wq, wk, wv, *[table] * groups)


def attend_kernel(at, place, q_ref, kv0, kv1, kv2, start_ref, out_ref):
    rows = q_ref.shape[0]
    chip, core = place[0], place[1]

    def index(block, axis):
        local = lax.broadcasted_iota(jnp.int32, (rows, rows), axis)
        local = lax.rem(local + core * (rows // 2), rows)
        return lax.rem(chip + (block % 4), 4) * rows + local

    query_at = index(at, 0)
    start = start_ref[:, :1].astype(jnp.int32)
    bias = []
    for block in (at, at - 1, at - 2):
        key_at = index(block, 1)
        allowed = (key_at <= query_at) & (key_at >= start)
        bias.append(jnp.where(allowed, F32(0.0), F32(-1e30)))
    bias = jnp.concatenate(bias, axis=1)
    keys = jnp.concatenate([kv0[:, :HD], kv1[:, :HD], kv2[:, :HD]], axis=0)
    values = jnp.concatenate([kv0[:, HD:], kv1[:, HD:], kv2[:, HD:]], axis=0)
    tile = rows
    for head in range(0, q_ref.shape[1], HD):
        for row in range(0, rows, tile):
            scores = lax.dot_general(
                q_ref[row : row + tile, head : head + HD],
                keys,
                (((1,), (1,)), ((), ())),
                preferred_element_type=F32,
            )
            scores = scores * F32(math.log2(math.e) / math.sqrt(HD)) + bias[row : row + tile]
            top = jnp.max(scores, axis=-1, keepdims=True)
            expo = jnp.exp2(scores - top)
            total = jnp.sum(expo, axis=-1, keepdims=True)
            context = jnp.dot(expo.astype(BF16), values, preferred_element_type=F32)
            out_ref[row : row + tile, head : head + HD] = (context / total).astype(BF16)


def attend(at, place, blocks, table):
    rows = blocks[0].shape[0]
    width = blocks[0].shape[1] - 2 * HD
    query = pl.BlockSpec((rows, width), lambda h, place: (0, 0))
    pair = pl.BlockSpec((rows, 2 * HD), lambda h, place: (0, width // (2 * HD)))
    return pl.pallas_call(
        functools.partial(attend_kernel, at),
        grid_spec=pltpu.PrefetchScalarGridSpec(
            num_scalar_prefetch=1,
            grid=(1,),
            in_specs=[query]
            + [pair] * 3
            + [pl.BlockSpec((None, rows, HD), lambda h, place: (at, 0, 2))],
            out_specs=query,
        ),
        out_shape=jax.ShapeDtypeStruct((rows, width), BF16),
        compiler_params=params(58),
        cost_estimate=cost(12 * rows * rows * width, 8 * rows * width, 12 * rows * rows),
        name="attend",
    )(place, blocks[0], blocks[0], blocks[1], blocks[2], table)


def times(own, other, low, high):
    half = own.shape[0] // 2
    turned = jnp.concatenate([other[half:, :], other[:half, :]], axis=0)
    total = jnp.dot(own[...], low, preferred_element_type=F32)
    return total + jnp.dot(turned, high, preferred_element_type=F32)


def joined(far, r, e):
    return jnp.concatenate([far[p, r, e] for p in range(far.shape[0])], axis=1)


def near_kernel(o0, t0, o3, t3, near_own, near_other, far, total_ref):
    total = times(o0, t0, near_own[...], near_other[...])
    total_ref[...] = total + times(o3, t3, joined(far, 0, 0), joined(far, 0, 1))


def project_near(o0, t0, o3, t3, near_own, near_other, far):
    rows, depth = o0.shape
    width, tile, piece = near_own.shape[1], 512, far.shape[-1]
    whole = pl.BlockSpec((rows, depth), lambda n: (0, 0))
    near = pl.BlockSpec((depth, tile), lambda n: (0, n))
    away = pl.BlockSpec((tile // piece, 1, 2, depth, piece), lambda n: (n, 2, 0, 0, 0))
    return pl.pallas_call(
        near_kernel,
        grid=(width // tile,),
        in_specs=[whole] * 4 + [near] * 2 + [away],
        out_specs=pl.BlockSpec((rows, tile), lambda n: (0, n)),
        out_shape=jax.ShapeDtypeStruct((rows, width), F32),
        compiler_params=params(58),
        cost_estimate=cost(8 * rows * depth * width, 8 * depth * width),
        name="project_near",
    )(o0, t0, o3, t3, near_own, near_other, far)


def out_kernel(o1, o2, t1, t2, far, total_ref, res_own, res_other, out_own, out_other):
    half = res_own.shape[0]
    total = total_ref[...] + times(o1, t1, joined(far, 0, 0), joined(far, 0, 1))
    total = total + times(o2, t2, joined(far, 1, 0), joined(far, 1, 1))
    out_own[...] = (res_own[...].astype(F32) + total[:half]).astype(BF16)
    out_other[...] = (res_other[...].astype(F32) + total[half:]).astype(BF16)


def project_out(own, other, far, total, res_own, res_other):
    rows, depth = own[0].shape
    half, width = res_own.shape
    tile, piece = 512, far.shape[-1]
    whole = pl.BlockSpec((rows, depth), lambda n: (0, 0))
    away = pl.BlockSpec((tile // piece, 2, 2, depth, piece), lambda n: (n, 0, 0, 0, 0))
    flat = pl.BlockSpec((half, tile), lambda n: (0, n))
    out = jax.ShapeDtypeStruct((half, width), BF16)
    return pl.pallas_call(
        out_kernel,
        grid=(width // tile,),
        in_specs=[whole] * 4 + [away, pl.BlockSpec((rows, tile), lambda n: (0, n))] + [flat] * 2,
        out_specs=[flat, flat],
        out_shape=[out, out],
        compiler_params=params(58),
        cost_estimate=cost(2 * rows * 4 * depth * width, 8 * depth * width),
        name="project_out",
    )(*own, *other, far, total, res_own, res_other)


def join_kernel(place, own_ref, back_ref, out_ref):
    @pl.when(pl.program_id(0) == 0)
    def _():
        out_ref[...] = own_ref[...]

    @pl.when(pl.program_id(0) == 1)
    def _():
        out_ref[...] = back_ref[...]


def join(place, own, back):
    rows, width = own.shape
    whole = pl.BlockSpec((rows, width), lambda n, place: (0, 0))
    return pl.pallas_call(
        join_kernel,
        grid_spec=pltpu.PrefetchScalarGridSpec(
            num_scalar_prefetch=1,
            grid=(2,),
            in_specs=[whole, whole],
            out_specs=pl.BlockSpec(
                (rows, width), lambda n, place: (0, lax.rem(place[1] + n, 2))
            ),
        ),
        out_shape=jax.ShapeDtypeStruct((rows, 2 * width), BF16),
        compiler_params=params(58),
        cost_estimate=cost(0, 8 * rows * width),
        name="join",
    )(place, own, back)


def local(residual, norm_gain, doc_ids, w_query, w_key, w_value, w_out):
    length = doc_ids.shape[0]
    rows, features = residual.shape
    n_z, chip_rows = 4, 2 * rows
    zh, core = lax.axis_index("zh"), lax.axis_index("c")
    column = lax.axis_index("x") * 4 + lax.axis_index("y")
    half = features // 2
    piece = half // 16

    def move(value, by, swap=0):
        perm = [
            (2 * z + c, 2 * ((z + by) % n_z) + (c ^ swap)) for z in range(n_z) for c in range(2)
        ]
        return lax.ppermute(value, ("zh", "c"), perm)

    def swap(value):
        return move(value, 0, 1)

    keep = lax.dynamic_slice_in_dim(w_out, core * half + column * piece, piece, 1)
    give = lax.dynamic_slice_in_dim(w_out, (1 - core) * half + column * piece, piece, 1)
    near = jnp.stack([keep, swap(give)])
    first, second = norm(residual, norm_gain)
    near, first, second = lax.optimization_barrier((near, first, second))
    far = lax.all_gather(jnp.stack([move(near, -r) for r in (1, 2, 3)]), ("x", "y"), axis=0)

    def relative(values):
        turned = lax.dynamic_slice_in_dim(
            jnp.concatenate([values, values]), zh * chip_rows, length, 0
        ).reshape(n_z, 2, rows)
        return jnp.where(core == 0, turned, turned[:, ::-1]).reshape(n_z, chip_rows)

    documents = relative(doc_ids)
    start = jnp.sum((doc_ids < documents[:, :, None]).astype(jnp.int32), axis=-1)
    chips = (zh + jnp.arange(n_z, dtype=jnp.int32)) % n_z
    cores = core ^ jnp.arange(2, dtype=jnp.int32)
    at = (2 * chips[:, None] + cores)[:, :, None] * rows + jnp.arange(rows, dtype=jnp.int32)
    at = at.reshape(n_z, chip_rows)
    freq = ROPE_BASE ** (-jnp.arange(HD // 2, dtype=F32) / (HD // 2))
    angle = (at - start).astype(F32)[:, :, None] * freq
    cosine, sine = jnp.cos(angle), jnp.sin(angle)
    wide = jnp.broadcast_to(start.astype(F32)[:, :, None], (n_z, chip_rows, HD))
    table = jnp.concatenate([cosine, cosine, -sine, sine, wide, wide], axis=-1)
    place = jnp.concatenate([zh[None], core[None]])

    def heads(blocks, *halves):
        pieces = []
        for a, b in halves:
            pieces += [a, b, swap(a), swap(b)]
        return project(pieces, w_query, w_key, w_value, table, blocks)

    qkv = [None] * 4
    up_first, down_second = move(first, 1), move(second, -1)
    up_second, down_first = move(second, 1), move(first, -1)
    (qkv[0],) = heads((0,), (first, second))
    far_first, far_second = move(up_first, 1), move(down_second, -1)
    up_first, up_second, down_first, down_second, qkv[0] = lax.optimization_barrier(
        (up_first, up_second, down_first, down_second, qkv[0])
    )
    qkv[3], qkv[1] = heads((3, 1), (up_first, up_second), (down_first, down_second))

    own, other = [None] * 4, [None] * 4

    def context(r):
        return attend(r, place, [qkv[r], qkv[(r - 1) % 4], qkv[(r - 2) % 4]], table)

    own[3] = move(context(1), 1)
    far_first, far_second, own[3] = lax.optimization_barrier((far_first, far_second, own[3]))
    (qkv[2],) = heads((2,), (far_first, far_second))
    own[2] = move(context(2), 2)
    sent = context(3)
    own[1] = move(sent, 3)
    qkv[0], sent = lax.optimization_barrier((qkv[0], sent))
    own[0] = context(0)
    other[3], other[0] = swap(own[3]), swap(own[0])

    near_own = lax.dynamic_slice_in_dim(w_out, core * half, half, 1)
    near_other = swap(lax.dynamic_slice_in_dim(w_out, (1 - core) * half, half, 1))
    res_own = lax.dynamic_slice_in_dim(residual, core * half, half, 1)
    res_other = swap(lax.dynamic_slice_in_dim(residual, (1 - core) * half, half, 1))
    total = project_near(own[0], other[0], own[3], other[3], near_own, near_other, far)
    own[1], own[2], total = lax.optimization_barrier((own[1], own[2], total))
    other[1], other[2] = swap(own[1]), swap(own[2])
    out_own, out_other = project_out(own[1:3], other[1:3], far, total, res_own, res_other)
    return join(place, out_own, swap(out_other))


def solution(mesh):
    fine = Mesh(mesh.devices.reshape(4, 4, 2, 4, 2), ALL)
    seq, tensor = ("x", "y", "zl"), ("zh", "c")
    placed = (
        P(ALL, None),
        P(),
        P(seq),
        P(None, tensor),
        P(None, tensor),
        P(None, tensor),
        P(tensor, None),
    )
    return jax.shard_map(local, mesh=fine, in_specs=placed, out_specs=P(ALL, None), check_vma=False)
```

```python
import functools
import math

import jax
import jax.numpy as jnp
from jax import lax
from jax.experimental import pallas as pl
from jax.experimental.pallas import tpu as pltpu
from jax.sharding import Mesh, PartitionSpec as P

HD = 128
ROPE_BASE = 500000.0
MIB = 1024 * 1024
F32 = jnp.float32
BF16 = jnp.bfloat16
ALL = ("x", "y", "zl", "zh", "c")


def params(mib):
    return pltpu.CompilerParams(vmem_limit_bytes=mib * MIB)


def cost(flops, bytes_accessed, transcendentals=0):
    return pl.CostEstimate(
        flops=int(flops), bytes_accessed=int(bytes_accessed), transcendentals=int(transcendentals)
    )


def norm_kernel(rows_ref, gain_ref, first_ref, second_ref):
    half = first_ref.shape[0]
    for at, out_ref in ((0, first_ref), (half, second_ref)):
        wide = rows_ref[at : at + half, :].astype(F32)
        scale = lax.rsqrt(jnp.mean(wide * wide, axis=-1, keepdims=True) + 1e-05)
        out_ref[...] = (wide * scale * gain_ref[...]).astype(BF16)


def norm(residual, gain):
    rows, width = residual.shape
    half = jax.ShapeDtypeStruct((rows // 2, width), BF16)
    return pl.pallas_call(
        norm_kernel,
        out_shape=(half, half),
        compiler_params=params(58),
        cost_estimate=cost(4 * rows * width, 4 * rows * width),
        name="norm",
    )(residual, gain.reshape(1, width))


def qkv_kernel(count, *refs):
    pieces, (wq, wk, wv) = refs[:count], refs[count : count + 3]
    groups = count // 4
    tables = refs[count + 3 : count + 3 + groups]
    outs = refs[count + 3 + groups : count + 3 + 2 * groups]
    lhs, weights, lhs_sem, sems = refs[count + 3 + 2 * groups :]
    piece = pieces[0].shape[0]
    rows = 4 * piece
    width = wq.shape[1]
    pair = 2 * HD
    first = [
        pltpu.make_async_copy(part, lhs.at[pl.ds(at * piece, piece), :], lhs_sem.at[at])
        for at, part in enumerate(pieces)
    ]
    loads = [
        [
            pltpu.make_async_copy(wk, weights.at[0, :, pl.ds(0, HD)], sems.at[0]),
            pltpu.make_async_copy(wv, weights.at[0, :, pl.ds(HD, HD)], sems.at[1]),
        ]
    ]
    for at in range(width // pair):
        part = wq.at[:, pl.ds(at * pair, pair)]
        loads.append([pltpu.make_async_copy(part, weights.at[at + 1], sems.at[at + 2])])
    for copy in first + loads[0] + loads[1]:
        copy.start()
    for copy in first:
        copy.wait()
    for step, group in enumerate(loads):
        for copy in group:
            copy.wait()
        if step and step + 1 < len(loads):
            for copy in loads[step + 1]:
                copy.start()
        for block in range(groups):
            table, out_ref = tables[block], outs[block]
            cosine, sine = table[:, :HD], table[:, HD : 2 * HD]

            def turn(part):
                return (part * cosine + pltpu.roll(part, HD // 2, 1) * sine).astype(BF16)

            product = jnp.dot(
                lhs[block * rows : (block + 1) * rows, :],
                weights[step],
                preferred_element_type=F32,
            )
            if step == 0:
                out_ref[:, width : width + HD] = turn(product[:, :HD])
                out_ref[:, width + HD :] = product[:, HD:].astype(BF16)
            else:
                at = (step - 1) * pair
                out_ref[:, at : at + HD] = turn(product[:, :HD])
                out_ref[:, at + HD : at + pair] = turn(product[:, HD:])


def project(pieces, wq, wk, wv, table, blocks):
    piece_rows, depth = pieces[0].shape
    count, groups = len(pieces), len(blocks)
    rows = piece_rows * 4
    width = wq.shape[1] + 2 * HD
    steps = width // (2 * HD)
    anywhere = pl.BlockSpec(memory_space=pl.ANY)

    def angles(at):
        return pl.BlockSpec((None, rows, 2 * HD), lambda k: (at, 0, 0))

    out = jax.ShapeDtypeStruct((rows, width), BF16)
    return pl.pallas_call(
        functools.partial(qkv_kernel, count),
        grid=(1,),
        in_specs=[anywhere] * (count + 3) + [angles(at) for at in blocks],
        out_specs=[pl.BlockSpec((rows, width), lambda k: (0, 0))] * groups,
        out_shape=[out] * groups,
        scratch_shapes=[
            pltpu.VMEM((rows * groups, depth), BF16),
            pltpu.VMEM((steps, depth, 2 * HD), BF16),
            pltpu.SemaphoreType.DMA((count,)),
            pltpu.SemaphoreType.DMA((steps + 1,)),
        ],
        compiler_params=params(58),
        cost_estimate=cost(2 * rows * groups * depth * width, 2 * depth * (rows * groups + width)),
        name="project",
    )(*pieces, wq, wk, wv, *[table] * groups)


def attend_kernel(at, place, q_ref, kv0, kv1, kv2, start_ref, out_ref):
    rows = q_ref.shape[0]
    chip, core = place[0], place[1]

    def index(block, axis):
        local = lax.broadcasted_iota(jnp.int32, (rows, rows), axis)
        local = lax.rem(local + core * (rows // 2), rows)
        return lax.rem(chip + (block % 4), 4) * rows + local

    query_at = index(at, 0)
    start = start_ref[:, :1].astype(jnp.int32)
    bias = []
    for block in (at, at - 1, at - 2):
        key_at = index(block, 1)
        allowed = (key_at <= query_at) & (key_at >= start)
        bias.append(jnp.where(allowed, F32(0.0), F32(-1e30)))
    bias = jnp.concatenate(bias, axis=1)
    keys = jnp.concatenate([kv0[:, :HD], kv1[:, :HD], kv2[:, :HD]], axis=0)
    values = jnp.concatenate([kv0[:, HD:], kv1[:, HD:], kv2[:, HD:]], axis=0)
    tile = rows
    for head in range(0, q_ref.shape[1], HD):
        for row in range(0, rows, tile):
            scores = lax.dot_general(
                q_ref[row : row + tile, head : head + HD],
                keys,
                (((1,), (1,)), ((), ())),
                preferred_element_type=F32,
            )
            scores = scores * F32(math.log2(math.e) / math.sqrt(HD)) + bias[row : row + tile]
            top = jnp.max(scores, axis=-1, keepdims=True)
            expo = jnp.exp2(scores - top)
            total = jnp.sum(expo, axis=-1, keepdims=True)
            context = jnp.dot(expo.astype(BF16), values, preferred_element_type=F32)
            out_ref[row : row + tile, head : head + HD] = (context / total).astype(BF16)


def attend(at, place, blocks, table):
    rows = blocks[0].shape[0]
    width = blocks[0].shape[1] - 2 * HD
    query = pl.BlockSpec((rows, width), lambda h, place: (0, 0))
    pair = pl.BlockSpec((rows, 2 * HD), lambda h, place: (0, width // (2 * HD)))
    return pl.pallas_call(
        functools.partial(attend_kernel, at),
        grid_spec=pltpu.PrefetchScalarGridSpec(
            num_scalar_prefetch=1,
            grid=(1,),
            in_specs=[query]
            + [pair] * 3
            + [pl.BlockSpec((None, rows, HD), lambda h, place: (at, 0, 2))],
            out_specs=query,
        ),
        out_shape=jax.ShapeDtypeStruct((rows, width), BF16),
        compiler_params=params(58),
        cost_estimate=cost(12 * rows * rows * width, 8 * rows * width, 12 * rows * rows),
        name="attend",
    )(place, blocks[0], blocks[0], blocks[1], blocks[2], table)


def times(own, other, low, high):
    half = own.shape[0] // 2
    turned = jnp.concatenate([other[half:, :], other[:half, :]], axis=0)
    total = jnp.dot(own[...], low, preferred_element_type=F32)
    return total + jnp.dot(turned, high, preferred_element_type=F32)


def joined(far, r, e):
    return jnp.concatenate([far[p, r, e] for p in range(far.shape[0])], axis=1)


def near_kernel(o0, t0, o3, t3, near_own, near_other, far, total_ref):
    total = times(o0, t0, near_own[...], near_other[...])
    total_ref[...] = total + times(o3, t3, joined(far, 0, 0), joined(far, 0, 1))


def project_near(o0, t0, o3, t3, near_own, near_other, far):
    rows, depth = o0.shape
    width, tile, piece = near_own.shape[1], 512, far.shape[-1]
    whole = pl.BlockSpec((rows, depth), lambda n: (0, 0))
    near = pl.BlockSpec((depth, tile), lambda n: (0, n))
    away = pl.BlockSpec((tile // piece, 1, 2, depth, piece), lambda n: (n, 2, 0, 0, 0))
    return pl.pallas_call(
        near_kernel,
        grid=(width // tile,),
        in_specs=[whole] * 4 + [near] * 2 + [away],
        out_specs=pl.BlockSpec((rows, tile), lambda n: (0, n)),
        out_shape=jax.ShapeDtypeStruct((rows, width), F32),
        compiler_params=params(58),
        cost_estimate=cost(8 * rows * depth * width, 8 * depth * width),
        name="project_near",
    )(o0, t0, o3, t3, near_own, near_other, far)


def out_kernel(o1, o2, t1, t2, far, total_ref, res_own, res_other, out_own, out_other):
    half = res_own.shape[0]
    total = total_ref[...] + times(o1, t1, joined(far, 0, 0), joined(far, 0, 1))
    total = total + times(o2, t2, joined(far, 1, 0), joined(far, 1, 1))
    out_own[...] = (res_own[...].astype(F32) + total[:half]).astype(BF16)
    out_other[...] = (res_other[...].astype(F32) + total[half:]).astype(BF16)


def project_out(own, other, far, total, res_own, res_other):
    rows, depth = own[0].shape
    half, width = res_own.shape
    tile, piece = 512, far.shape[-1]
    whole = pl.BlockSpec((rows, depth), lambda n: (0, 0))
    away = pl.BlockSpec((tile // piece, 2, 2, depth, piece), lambda n: (n, 0, 0, 0, 0))
    flat = pl.BlockSpec((half, tile), lambda n: (0, n))
    out = jax.ShapeDtypeStruct((half, width), BF16)
    return pl.pallas_call(
        out_kernel,
        grid=(width // tile,),
        in_specs=[whole] * 4 + [away, pl.BlockSpec((rows, tile), lambda n: (0, n))] + [flat] * 2,
        out_specs=[flat, flat],
        out_shape=[out, out],
        compiler_params=params(58),
        cost_estimate=cost(2 * rows * 4 * depth * width, 8 * depth * width),
        name="project_out",
    )(*own, *other, far, total, res_own, res_other)


def join_kernel(place, own_ref, back_ref, out_ref):
    @pl.when(pl.program_id(0) == 0)
    def _():
        out_ref[...] = own_ref[...]

    @pl.when(pl.program_id(0) == 1)
    def _():
        out_ref[...] = back_ref[...]


def join(place, own, back):
    rows, width = own.shape
    whole = pl.BlockSpec((rows, width), lambda n, place: (0, 0))
    return pl.pallas_call(
        join_kernel,
        grid_spec=pltpu.PrefetchScalarGridSpec(
            num_scalar_prefetch=1,
            grid=(2,),
            in_specs=[whole, whole],
            out_specs=pl.BlockSpec(
                (rows, width), lambda n, place: (0, lax.rem(place[1] + n, 2))
            ),
        ),
        out_shape=jax.ShapeDtypeStruct((rows, 2 * width), BF16),
        compiler_params=params(58),
        cost_estimate=cost(0, 8 * rows * width),
        name="join",
    )(place, own, back)


def local(residual, norm_gain, doc_ids, w_query, w_key, w_value, w_out):
    length = doc_ids.shape[0]
    rows, features = residual.shape
    n_z, chip_rows = 4, 2 * rows
    zh, core = lax.axis_index("zh"), lax.axis_index("c")
    column = lax.axis_index("x") * 4 + lax.axis_index("y")
    half = features // 2
    piece = half // 16

    def move(value, by, swap=0):
        perm = [
            (2 * z + c, 2 * ((z + by) % n_z) + (c ^ swap)) for z in range(n_z) for c in range(2)
        ]
        return lax.ppermute(value, ("zh", "c"), perm)

    def swap(value):
        return move(value, 0, 1)

    keep = lax.dynamic_slice_in_dim(w_out, core * half + column * piece, piece, 1)
    give = lax.dynamic_slice_in_dim(w_out, (1 - core) * half + column * piece, piece, 1)
    near = jnp.stack([keep, swap(give)])
    first, second = norm(residual, norm_gain)
    near, first, second = lax.optimization_barrier((near, first, second))
    up_first, down_second = move(first, 1), move(second, -1)
    shifted = [move(near, -r) for r in (1, 2, 3)]
    *shifted, up_first, down_second = lax.optimization_barrier((*shifted, up_first, down_second))
    far = lax.all_gather(jnp.stack(shifted), ("x", "y"), axis=0)

    def relative(values):
        turned = lax.dynamic_slice_in_dim(
            jnp.concatenate([values, values]), zh * chip_rows, length, 0
        ).reshape(n_z, 2, rows)
        return jnp.where(core == 0, turned, turned[:, ::-1]).reshape(n_z, chip_rows)

    documents = relative(doc_ids)
    start = jnp.sum((doc_ids < documents[:, :, None]).astype(jnp.int32), axis=-1)
    chips = (zh + jnp.arange(n_z, dtype=jnp.int32)) % n_z
    cores = core ^ jnp.arange(2, dtype=jnp.int32)
    at = (2 * chips[:, None] + cores)[:, :, None] * rows + jnp.arange(rows, dtype=jnp.int32)
    at = at.reshape(n_z, chip_rows)
    freq = ROPE_BASE ** (-jnp.arange(HD // 2, dtype=F32) / (HD // 2))
    angle = (at - start).astype(F32)[:, :, None] * freq
    cosine, sine = jnp.cos(angle), jnp.sin(angle)
    wide = jnp.broadcast_to(start.astype(F32)[:, :, None], (n_z, chip_rows, HD))
    table = jnp.concatenate([cosine, cosine, -sine, sine, wide, wide], axis=-1)
    place = jnp.concatenate([zh[None], core[None]])

    def heads(blocks, *halves):
        pieces = []
        for a, b in halves:
            pieces += [a, b, swap(a), swap(b)]
        return project(pieces, w_query, w_key, w_value, table, blocks)

    qkv = [None] * 4
    up_second, down_first = move(second, 1), move(first, -1)
    (qkv[0],) = heads((0,), (first, second))
    far_first, far_second = move(up_first, 1), move(down_second, -1)
    up_first, up_second, down_first, down_second, qkv[0] = lax.optimization_barrier(
        (up_first, up_second, down_first, down_second, qkv[0])
    )
    qkv[3], qkv[1] = heads((3, 1), (up_first, up_second), (down_first, down_second))

    own, other = [None] * 4, [None] * 4

    def context(r):
        return attend(r, place, [qkv[r], qkv[(r - 1) % 4], qkv[(r - 2) % 4]], table)

    own[3] = move(context(1), 1)
    far_first, far_second, own[3] = lax.optimization_barrier((far_first, far_second, own[3]))
    (qkv[2],) = heads((2,), (far_first, far_second))
    own[2] = move(context(2), 2)
    sent = context(3)
    own[1] = move(sent, 3)
    qkv[0], sent = lax.optimization_barrier((qkv[0], sent))
    own[0] = context(0)
    other[3], other[0] = swap(own[3]), swap(own[0])

    near_own = lax.dynamic_slice_in_dim(w_out, core * half, half, 1)
    near_other = swap(lax.dynamic_slice_in_dim(w_out, (1 - core) * half, half, 1))
    res_own = lax.dynamic_slice_in_dim(residual, core * half, half, 1)
    res_other = swap(lax.dynamic_slice_in_dim(residual, (1 - core) * half, half, 1))
    total = project_near(own[0], other[0], own[3], other[3], near_own, near_other, far)
    own[1], own[2], total = lax.optimization_barrier((own[1], own[2], total))
    other[1], other[2] = swap(own[1]), swap(own[2])
    out_own, out_other = project_out(own[1:3], other[1:3], far, total, res_own, res_other)
    return join(place, out_own, swap(out_other))


def solution(mesh):
    fine = Mesh(mesh.devices.reshape(4, 4, 2, 4, 2), ALL)
    seq, tensor = ("x", "y", "zl"), ("zh", "c")
    placed = (
        P(ALL, None),
        P(),
        P(seq),
        P(None, tensor),
        P(None, tensor),
        P(None, tensor),
        P(tensor, None),
    )
    return jax.shard_map(local, mesh=fine, in_specs=placed, out_specs=P(ALL, None), check_vma=False)
```

```python
import functools
import math

import jax
import jax.numpy as jnp
from jax import lax
from jax.experimental import pallas as pl
from jax.experimental.pallas import tpu as pltpu
from jax.sharding import Mesh, PartitionSpec as P

HD = 128
ROPE_BASE = 500000.0
MIB = 1024 * 1024
F32 = jnp.float32
BF16 = jnp.bfloat16
ALL = ("x", "y", "zl", "zh", "c")


def params(mib):
    return pltpu.CompilerParams(vmem_limit_bytes=mib * MIB)


def cost(flops, bytes_accessed, transcendentals=0):
    return pl.CostEstimate(
        flops=int(flops), bytes_accessed=int(bytes_accessed), transcendentals=int(transcendentals)
    )


def norm_kernel(rows_ref, gain_ref, first_ref, second_ref):
    half = first_ref.shape[0]
    for at, out_ref in ((0, first_ref), (half, second_ref)):
        wide = rows_ref[at : at + half, :].astype(F32)
        scale = lax.rsqrt(jnp.mean(wide * wide, axis=-1, keepdims=True) + 1e-05)
        out_ref[...] = (wide * scale * gain_ref[...]).astype(BF16)


def norm(residual, gain):
    rows, width = residual.shape
    half = jax.ShapeDtypeStruct((rows // 2, width), BF16)
    return pl.pallas_call(
        norm_kernel,
        out_shape=(half, half),
        compiler_params=params(58),
        cost_estimate=cost(4 * rows * width, 4 * rows * width),
        name="norm",
    )(residual, gain.reshape(1, width))


def qkv_kernel(count, *refs):
    pieces, (wq, wk, wv) = refs[:count], refs[count : count + 3]
    groups = count // 4
    tables = refs[count + 3 : count + 3 + groups]
    outs = refs[count + 3 + groups : count + 3 + 2 * groups]
    lhs, weights, lhs_sem, sems = refs[count + 3 + 2 * groups :]
    piece = pieces[0].shape[0]
    rows = 4 * piece
    width = wq.shape[1]
    pair = 2 * HD
    first = [
        pltpu.make_async_copy(part, lhs.at[pl.ds(at * piece, piece), :], lhs_sem.at[at])
        for at, part in enumerate(pieces)
    ]
    loads = [
        [
            pltpu.make_async_copy(wk, weights.at[0, :, pl.ds(0, HD)], sems.at[0]),
            pltpu.make_async_copy(wv, weights.at[0, :, pl.ds(HD, HD)], sems.at[1]),
        ]
    ]
    for at in range(width // pair):
        part = wq.at[:, pl.ds(at * pair, pair)]
        loads.append([pltpu.make_async_copy(part, weights.at[at + 1], sems.at[at + 2])])
    for copy in first + loads[0] + loads[1]:
        copy.start()
    for copy in first:
        copy.wait()
    for step, group in enumerate(loads):
        for copy in group:
            copy.wait()
        if step and step + 1 < len(loads):
            for copy in loads[step + 1]:
                copy.start()
        for block in range(groups):
            table, out_ref = tables[block], outs[block]
            cosine, sine = table[:, :HD], table[:, HD : 2 * HD]

            def turn(part):
                return (part * cosine + pltpu.roll(part, HD // 2, 1) * sine).astype(BF16)

            product = jnp.dot(
                lhs[block * rows : (block + 1) * rows, :],
                weights[step],
                preferred_element_type=F32,
            )
            if step == 0:
                out_ref[:, width : width + HD] = turn(product[:, :HD])
                out_ref[:, width + HD :] = product[:, HD:].astype(BF16)
            else:
                at = (step - 1) * pair
                out_ref[:, at : at + HD] = turn(product[:, :HD])
                out_ref[:, at + HD : at + pair] = turn(product[:, HD:])


def project(pieces, wq, wk, wv, table, blocks):
    piece_rows, depth = pieces[0].shape
    count, groups = len(pieces), len(blocks)
    rows = piece_rows * 4
    width = wq.shape[1] + 2 * HD
    steps = width // (2 * HD)
    anywhere = pl.BlockSpec(memory_space=pl.ANY)

    def angles(at):
        return pl.BlockSpec((None, rows, 2 * HD), lambda k: (at, 0, 0))

    out = jax.ShapeDtypeStruct((rows, width), BF16)
    return pl.pallas_call(
        functools.partial(qkv_kernel, count),
        grid=(1,),
        in_specs=[anywhere] * (count + 3) + [angles(at) for at in blocks],
        out_specs=[pl.BlockSpec((rows, width), lambda k: (0, 0))] * groups,
        out_shape=[out] * groups,
        scratch_shapes=[
            pltpu.VMEM((rows * groups, depth), BF16),
            pltpu.VMEM((steps, depth, 2 * HD), BF16),
            pltpu.SemaphoreType.DMA((count,)),
            pltpu.SemaphoreType.DMA((steps + 1,)),
        ],
        compiler_params=params(58),
        cost_estimate=cost(2 * rows * groups * depth * width, 2 * depth * (rows * groups + width)),
        name="project",
    )(*pieces, wq, wk, wv, *[table] * groups)


def attend_kernel(at, place, q_ref, kv0, kv1, kv2, start_ref, out_ref):
    rows = q_ref.shape[0]
    chip, core = place[0], place[1]

    def index(block, axis):
        local = lax.broadcasted_iota(jnp.int32, (rows, rows), axis)
        local = lax.rem(local + core * (rows // 2), rows)
        return lax.rem(chip + (block % 4), 4) * rows + local

    query_at = index(at, 0)
    start = start_ref[:, :1].astype(jnp.int32)
    bias = []
    for block in (at, at - 1, at - 2):
        key_at = index(block, 1)
        allowed = (key_at <= query_at) & (key_at >= start)
        bias.append(jnp.where(allowed, F32(0.0), F32(-1e30)))
    bias = jnp.concatenate(bias, axis=1)
    keys = jnp.concatenate([kv0[:, :HD], kv1[:, :HD], kv2[:, :HD]], axis=0)
    values = jnp.concatenate([kv0[:, HD:], kv1[:, HD:], kv2[:, HD:]], axis=0)
    tile = rows
    for head in range(0, q_ref.shape[1], HD):
        for row in range(0, rows, tile):
            scores = lax.dot_general(
                q_ref[row : row + tile, head : head + HD],
                keys,
                (((1,), (1,)), ((), ())),
                preferred_element_type=F32,
            )
            scores = scores * F32(math.log2(math.e) / math.sqrt(HD)) + bias[row : row + tile]
            top = jnp.max(scores, axis=-1, keepdims=True)
            expo = jnp.exp2(scores - top)
            total = jnp.sum(expo, axis=-1, keepdims=True)
            context = jnp.dot(expo.astype(BF16), values, preferred_element_type=F32)
            out_ref[row : row + tile, head : head + HD] = (context / total).astype(BF16)


def attend(at, place, blocks, table):
    rows = blocks[0].shape[0]
    width = blocks[0].shape[1] - 2 * HD
    query = pl.BlockSpec((rows, width), lambda h, place: (0, 0))
    pair = pl.BlockSpec((rows, 2 * HD), lambda h, place: (0, width // (2 * HD)))
    return pl.pallas_call(
        functools.partial(attend_kernel, at),
        grid_spec=pltpu.PrefetchScalarGridSpec(
            num_scalar_prefetch=1,
            grid=(1,),
            in_specs=[query]
            + [pair] * 3
            + [pl.BlockSpec((None, rows, HD), lambda h, place: (at, 0, 2))],
            out_specs=query,
        ),
        out_shape=jax.ShapeDtypeStruct((rows, width), BF16),
        compiler_params=params(58),
        cost_estimate=cost(12 * rows * rows * width, 8 * rows * width, 12 * rows * rows),
        name="attend",
    )(place, blocks[0], blocks[0], blocks[1], blocks[2], table)


def times(own, other, low, high):
    half = own.shape[0] // 2
    turned = jnp.concatenate([other[half:, :], other[:half, :]], axis=0)
    total = jnp.dot(own[...], low, preferred_element_type=F32)
    return total + jnp.dot(turned, high, preferred_element_type=F32)


def joined(far, r, e):
    return jnp.concatenate([far[p, r, e] for p in range(far.shape[0])], axis=1)


def near_kernel(own, other, near_own, near_other, total_ref):
    total_ref[...] = times(own, other, near_own[...], near_other[...])


def project_near(own, other, near_own, near_other):
    rows, depth = own.shape
    width, tile = near_own.shape[1], 512
    whole = pl.BlockSpec((rows, depth), lambda n: (0, 0))
    near = pl.BlockSpec((depth, tile), lambda n: (0, n))
    return pl.pallas_call(
        near_kernel,
        grid=(width // tile,),
        in_specs=[whole] * 2 + [near] * 2,
        out_specs=pl.BlockSpec((rows, tile), lambda n: (0, n)),
        out_shape=jax.ShapeDtypeStruct((rows, width), F32),
        compiler_params=params(58),
        cost_estimate=cost(4 * rows * depth * width, 4 * depth * width),
        name="project_near",
    )(own, other, near_own, near_other)


def out_kernel(o1, o2, o3, t1, t2, t3, far, total_ref, res_own, res_other, out_own, out_other):
    half = res_own.shape[0]
    total = total_ref[...]
    for r, (own, other) in enumerate(((o1, t1), (o2, t2), (o3, t3))):
        total = total + times(own, other, joined(far, r, 0), joined(far, r, 1))
    out_own[...] = (res_own[...].astype(F32) + total[:half]).astype(BF16)
    out_other[...] = (res_other[...].astype(F32) + total[half:]).astype(BF16)


def project_out(own, other, far, total, res_own, res_other):
    rows, depth = own[0].shape
    half, width = res_own.shape
    tile, piece = 512, far.shape[-1]
    whole = pl.BlockSpec((rows, depth), lambda n: (0, 0))
    away = pl.BlockSpec((tile // piece, 3, 2, depth, piece), lambda n: (n, 0, 0, 0, 0))
    flat = pl.BlockSpec((half, tile), lambda n: (0, n))
    out = jax.ShapeDtypeStruct((half, width), BF16)
    return pl.pallas_call(
        out_kernel,
        grid=(width // tile,),
        in_specs=[whole] * 6 + [away, pl.BlockSpec((rows, tile), lambda n: (0, n))] + [flat] * 2,
        out_specs=[flat, flat],
        out_shape=[out, out],
        compiler_params=params(58),
        cost_estimate=cost(2 * rows * 6 * depth * width, 12 * depth * width),
        name="project_out",
    )(*own, *other, far, total, res_own, res_other)


def join_kernel(place, own_ref, back_ref, out_ref):
    @pl.when(pl.program_id(0) == 0)
    def _():
        out_ref[...] = own_ref[...]

    @pl.when(pl.program_id(0) == 1)
    def _():
        out_ref[...] = back_ref[...]


def join(place, own, back):
    rows, width = own.shape
    whole = pl.BlockSpec((rows, width), lambda n, place: (0, 0))
    return pl.pallas_call(
        join_kernel,
        grid_spec=pltpu.PrefetchScalarGridSpec(
            num_scalar_prefetch=1,
            grid=(2,),
            in_specs=[whole, whole],
            out_specs=pl.BlockSpec(
                (rows, width), lambda n, place: (0, lax.rem(place[1] + n, 2))
            ),
        ),
        out_shape=jax.ShapeDtypeStruct((rows, 2 * width), BF16),
        compiler_params=params(58),
        cost_estimate=cost(0, 8 * rows * width),
        name="join",
    )(place, own, back)


def local(residual, norm_gain, doc_ids, w_query, w_key, w_value, w_out):
    length = doc_ids.shape[0]
    rows, features = residual.shape
    n_z, chip_rows = 4, 2 * rows
    zh, core = lax.axis_index("zh"), lax.axis_index("c")
    column = lax.axis_index("x") * 4 + lax.axis_index("y")
    half = features // 2
    piece = half // 16

    def move(value, by, swap=0):
        perm = [
            (2 * z + c, 2 * ((z + by) % n_z) + (c ^ swap)) for z in range(n_z) for c in range(2)
        ]
        return lax.ppermute(value, ("zh", "c"), perm)

    def swap(value):
        return move(value, 0, 1)

    keep = lax.dynamic_slice_in_dim(w_out, core * half + column * piece, piece, 1)
    give = lax.dynamic_slice_in_dim(w_out, (1 - core) * half + column * piece, piece, 1)
    near = jnp.stack([keep, swap(give)])
    first, second = norm(residual, norm_gain)
    near, first, second = lax.optimization_barrier((near, first, second))
    up_first, down_second = move(first, 1), move(second, -1)
    shifted = [move(near, -r) for r in (1, 2, 3)]
    *shifted, up_first, down_second = lax.optimization_barrier((*shifted, up_first, down_second))
    far = lax.all_gather(jnp.stack(shifted), ("x", "y"), axis=0)

    def relative(values):
        turned = lax.dynamic_slice_in_dim(
            jnp.concatenate([values, values]), zh * chip_rows, length, 0
        ).reshape(n_z, 2, rows)
        return jnp.where(core == 0, turned, turned[:, ::-1]).reshape(n_z, chip_rows)

    documents = relative(doc_ids)
    start = jnp.sum((doc_ids < documents[:, :, None]).astype(jnp.int32), axis=-1)
    chips = (zh + jnp.arange(n_z, dtype=jnp.int32)) % n_z
    cores = core ^ jnp.arange(2, dtype=jnp.int32)
    at = (2 * chips[:, None] + cores)[:, :, None] * rows + jnp.arange(rows, dtype=jnp.int32)
    at = at.reshape(n_z, chip_rows)
    freq = ROPE_BASE ** (-jnp.arange(HD // 2, dtype=F32) / (HD // 2))
    angle = (at - start).astype(F32)[:, :, None] * freq
    cosine, sine = jnp.cos(angle), jnp.sin(angle)
    wide = jnp.broadcast_to(start.astype(F32)[:, :, None], (n_z, chip_rows, HD))
    table = jnp.concatenate([cosine, cosine, -sine, sine, wide, wide], axis=-1)
    place = jnp.concatenate([zh[None], core[None]])

    def heads(blocks, *halves):
        pieces = []
        for a, b in halves:
            pieces += [a, b, swap(a), swap(b)]
        return project(pieces, w_query, w_key, w_value, table, blocks)

    qkv = [None] * 4
    up_second, down_first = move(second, 1), move(first, -1)
    (qkv[0],) = heads((0,), (first, second))
    up_first, down_second, qkv[0] = lax.optimization_barrier((up_first, down_second, qkv[0]))
    far_first, far_second = move(up_first, 1), move(down_second, -1)
    qkv[3], qkv[1], qkv[2] = heads(
        (3, 1, 2), (up_first, up_second), (down_first, down_second), (far_first, far_second)
    )

    own = [None] * 4

    def context(r):
        return attend(r, place, [qkv[r], qkv[(r - 1) % 4], qkv[(r - 2) % 4]], table)

    own[2] = move(context(2), 2)
    sent = context(3)
    own[1] = move(sent, 3)
    sent = context(1)
    own[3] = move(sent, 1)
    qkv[0], own[2] = lax.optimization_barrier((qkv[0], own[2]))
    own[0] = context(0)
    other = [swap(part) for part in own]

    near_own = lax.dynamic_slice_in_dim(w_out, core * half, half, 1)
    near_other = swap(lax.dynamic_slice_in_dim(w_out, (1 - core) * half, half, 1))
    res_own = lax.dynamic_slice_in_dim(residual, core * half, half, 1)
    res_other = swap(lax.dynamic_slice_in_dim(residual, (1 - core) * half, half, 1))
    total = project_near(own[0], other[0], near_own, near_other)
    out_own, out_other = project_out(own[1:], other[1:], far, total, res_own, res_other)
    return join(place, out_own, swap(out_other))


def solution(mesh):
    fine = Mesh(mesh.devices.reshape(4, 4, 2, 4, 2), ALL)
    seq, tensor = ("x", "y", "zl"), ("zh", "c")
    placed = (
        P(ALL, None),
        P(),
        P(seq),
        P(None, tensor),
        P(None, tensor),
        P(None, tensor),
        P(tensor, None),
    )
    return jax.shard_map(local, mesh=fine, in_specs=placed, out_specs=P(ALL, None), check_vma=False)
```

```python
import functools
import math

import jax
import jax.numpy as jnp
from jax import lax
from jax.experimental import pallas as pl
from jax.experimental.pallas import tpu as pltpu
from jax.sharding import Mesh, PartitionSpec as P

HD = 128
ROPE_BASE = 500000.0
MIB = 1024 * 1024
F32 = jnp.float32
BF16 = jnp.bfloat16
ALL = ("x", "y", "zl", "zh", "c")


def params(mib):
    return pltpu.CompilerParams(vmem_limit_bytes=mib * MIB)


def cost(flops, bytes_accessed, transcendentals=0):
    return pl.CostEstimate(
        flops=int(flops), bytes_accessed=int(bytes_accessed), transcendentals=int(transcendentals)
    )


def norm_kernel(rows_ref, gain_ref, first_ref, second_ref):
    half = first_ref.shape[0]
    for at, out_ref in ((0, first_ref), (half, second_ref)):
        wide = rows_ref[at : at + half, :].astype(F32)
        scale = lax.rsqrt(jnp.mean(wide * wide, axis=-1, keepdims=True) + 1e-05)
        out_ref[...] = (wide * scale * gain_ref[...]).astype(BF16)


def norm(residual, gain):
    rows, width = residual.shape
    half = jax.ShapeDtypeStruct((rows // 2, width), BF16)
    return pl.pallas_call(
        norm_kernel,
        out_shape=(half, half),
        compiler_params=params(24),
        cost_estimate=cost(4 * rows * width, 4 * rows * width),
        name="norm",
    )(residual, gain.reshape(1, width))


def qkv_kernel(count, *refs):
    pieces, (wq, wk, wv) = refs[:count], refs[count : count + 3]
    groups = count // 4
    tables = refs[count + 3 : count + 3 + groups]
    outs = refs[count + 3 + groups : count + 3 + 2 * groups]
    lhs, weights, lhs_sem, sems = refs[count + 3 + 2 * groups :]
    piece = pieces[0].shape[0]
    rows = 4 * piece
    width = wq.shape[1]
    pair = 2 * HD
    first = [
        pltpu.make_async_copy(part, lhs.at[pl.ds(at * piece, piece), :], lhs_sem.at[at])
        for at, part in enumerate(pieces)
    ]
    loads = [
        [
            pltpu.make_async_copy(wk, weights.at[0, :, pl.ds(0, HD)], sems.at[0]),
            pltpu.make_async_copy(wv, weights.at[0, :, pl.ds(HD, HD)], sems.at[1]),
        ]
    ]
    for at in range(width // pair):
        part = wq.at[:, pl.ds(at * pair, pair)]
        loads.append([pltpu.make_async_copy(part, weights.at[at + 1], sems.at[at + 2])])
    for copy in first + loads[0] + loads[1]:
        copy.start()
    for copy in first:
        copy.wait()
    for step, group in enumerate(loads):
        for copy in group:
            copy.wait()
        if step and step + 1 < len(loads):
            for copy in loads[step + 1]:
                copy.start()
        for block in range(groups):
            table, out_ref = tables[block], outs[block]
            cosine, sine = table[:, :HD], table[:, HD : 2 * HD]

            def turn(part):
                return (part * cosine + pltpu.roll(part, HD // 2, 1) * sine).astype(BF16)

            product = jnp.dot(
                lhs[block * rows : (block + 1) * rows, :],
                weights[step],
                preferred_element_type=F32,
            )
            if step == 0:
                out_ref[:, width : width + HD] = turn(product[:, :HD])
                out_ref[:, width + HD :] = product[:, HD:].astype(BF16)
            else:
                at = (step - 1) * pair
                out_ref[:, at : at + HD] = turn(product[:, :HD])
                out_ref[:, at + HD : at + pair] = turn(product[:, HD:])


def project(pieces, wq, wk, wv, table, blocks):
    piece_rows, depth = pieces[0].shape
    count, groups = len(pieces), len(blocks)
    rows = piece_rows * 4
    width = wq.shape[1] + 2 * HD
    steps = width // (2 * HD)
    anywhere = pl.BlockSpec(memory_space=pl.ANY)

    def angles(at):
        return pl.BlockSpec((None, rows, 2 * HD), lambda k: (at, 0, 0))

    out = jax.ShapeDtypeStruct((rows, width), BF16)
    return pl.pallas_call(
        functools.partial(qkv_kernel, count),
        grid=(1,),
        in_specs=[anywhere] * (count + 3) + [angles(at) for at in blocks],
        out_specs=[pl.BlockSpec((rows, width), lambda k: (0, 0))] * groups,
        out_shape=[out] * groups,
        scratch_shapes=[
            pltpu.VMEM((rows * groups, depth), BF16),
            pltpu.VMEM((steps, depth, 2 * HD), BF16),
            pltpu.SemaphoreType.DMA((count,)),
            pltpu.SemaphoreType.DMA((steps + 1,)),
        ],
        compiler_params=params(58),
        cost_estimate=cost(2 * rows * groups * depth * width, 2 * depth * (rows * groups + width)),
        name="project",
    )(*pieces, wq, wk, wv, *[table] * groups)


def attend_kernel(at, place, q_ref, kv0, kv1, kv2, start_ref, out_ref):
    rows = q_ref.shape[0]
    chip, core = place[0], place[1]

    def index(block, axis):
        local = lax.broadcasted_iota(jnp.int32, (rows, rows), axis)
        local = lax.rem(local + core * (rows // 2), rows)
        return lax.rem(chip + (block % 4), 4) * rows + local

    query_at = index(at, 0)
    start = start_ref[:, :1].astype(jnp.int32)
    bias = []
    for block in (at, at - 1, at - 2):
        key_at = index(block, 1)
        allowed = (key_at <= query_at) & (key_at >= start)
        bias.append(jnp.where(allowed, F32(0.0), F32(-1e30)))
    bias = jnp.concatenate(bias, axis=1)
    keys = jnp.concatenate([kv0[:, :HD], kv1[:, :HD], kv2[:, :HD]], axis=0)
    values = jnp.concatenate([kv0[:, HD:], kv1[:, HD:], kv2[:, HD:]], axis=0)
    tile = rows
    for head in range(0, q_ref.shape[1], HD):
        for row in range(0, rows, tile):
            scores = lax.dot_general(
                q_ref[row : row + tile, head : head + HD],
                keys,
                (((1,), (1,)), ((), ())),
                preferred_element_type=F32,
            )
            scores = scores * F32(math.log2(math.e) / math.sqrt(HD)) + bias[row : row + tile]
            top = jnp.max(scores, axis=-1, keepdims=True)
            expo = jnp.exp2(scores - top)
            total = jnp.sum(expo, axis=-1, keepdims=True)
            context = jnp.dot(expo.astype(BF16), values, preferred_element_type=F32)
            out_ref[row : row + tile, head : head + HD] = (context / total).astype(BF16)


def attend(at, place, blocks, table):
    rows = blocks[0].shape[0]
    width = blocks[0].shape[1] - 2 * HD
    query = pl.BlockSpec((rows, width), lambda h, place: (0, 0))
    pair = pl.BlockSpec((rows, 2 * HD), lambda h, place: (0, width // (2 * HD)))
    return pl.pallas_call(
        functools.partial(attend_kernel, at),
        grid_spec=pltpu.PrefetchScalarGridSpec(
            num_scalar_prefetch=1,
            grid=(1,),
            in_specs=[query]
            + [pair] * 3
            + [pl.BlockSpec((None, rows, HD), lambda h, place: (at, 0, 2))],
            out_specs=query,
        ),
        out_shape=jax.ShapeDtypeStruct((rows, width), BF16),
        compiler_params=params(58),
        cost_estimate=cost(12 * rows * rows * width, 8 * rows * width, 12 * rows * rows),
        name="attend",
    )(place, blocks[0], blocks[0], blocks[1], blocks[2], table)


def times(own, other, low, high):
    half = own.shape[0] // 2
    turned = jnp.concatenate([other[half:, :], other[:half, :]], axis=0)
    total = jnp.dot(own[...], low, preferred_element_type=F32)
    return total + jnp.dot(turned, high, preferred_element_type=F32)


def joined(far, r, e):
    return jnp.concatenate([far[p, r, e] for p in range(far.shape[0])], axis=1)


def near_kernel(own, other, near_own, near_other, total_ref):
    total_ref[...] = times(own, other, near_own[...], near_other[...])


def project_near(own, other, near_own, near_other):
    rows, depth = own.shape
    width, tile = near_own.shape[1], 512
    whole = pl.BlockSpec((rows, depth), lambda n: (0, 0))
    near = pl.BlockSpec((depth, tile), lambda n: (0, n))
    return pl.pallas_call(
        near_kernel,
        grid=(width // tile,),
        in_specs=[whole] * 2 + [near] * 2,
        out_specs=pl.BlockSpec((rows, tile), lambda n: (0, n)),
        out_shape=jax.ShapeDtypeStruct((rows, width), F32),
        compiler_params=params(58),
        cost_estimate=cost(4 * rows * depth * width, 4 * depth * width),
        name="project_near",
    )(own, other, near_own, near_other)


def out_kernel(o1, o2, o3, t1, t2, t3, far, total_ref, res_own, res_other, out_own, out_other):
    half = res_own.shape[0]
    total = total_ref[...]
    for r, (own, other) in enumerate(((o1, t1), (o2, t2), (o3, t3))):
        total = total + times(own, other, joined(far, r, 0), joined(far, r, 1))
    out_own[...] = (res_own[...].astype(F32) + total[:half]).astype(BF16)
    out_other[...] = (res_other[...].astype(F32) + total[half:]).astype(BF16)


def project_out(own, other, far, total, res_own, res_other):
    rows, depth = own[0].shape
    half, width = res_own.shape
    tile, piece = 512, far.shape[-1]
    whole = pl.BlockSpec((rows, depth), lambda n: (0, 0))
    away = pl.BlockSpec((tile // piece, 3, 2, depth, piece), lambda n: (n, 0, 0, 0, 0))
    flat = pl.BlockSpec((half, tile), lambda n: (0, n))
    out = jax.ShapeDtypeStruct((half, width), BF16)
    return pl.pallas_call(
        out_kernel,
        grid=(width // tile,),
        in_specs=[whole] * 6 + [away, pl.BlockSpec((rows, tile), lambda n: (0, n))] + [flat] * 2,
        out_specs=[flat, flat],
        out_shape=[out, out],
        compiler_params=params(58),
        cost_estimate=cost(2 * rows * 6 * depth * width, 12 * depth * width),
        name="project_out",
    )(*own, *other, far, total, res_own, res_other)


def join_kernel(place, own_ref, back_ref, out_ref):
    @pl.when(pl.program_id(0) == 0)
    def _():
        out_ref[...] = own_ref[...]

    @pl.when(pl.program_id(0) == 1)
    def _():
        out_ref[...] = back_ref[...]


def join(place, own, back):
    rows, width = own.shape
    whole = pl.BlockSpec((rows, width), lambda n, place: (0, 0))
    return pl.pallas_call(
        join_kernel,
        grid_spec=pltpu.PrefetchScalarGridSpec(
            num_scalar_prefetch=1,
            grid=(2,),
            in_specs=[whole, whole],
            out_specs=pl.BlockSpec(
                (rows, width), lambda n, place: (0, lax.rem(place[1] + n, 2))
            ),
        ),
        out_shape=jax.ShapeDtypeStruct((rows, 2 * width), BF16),
        compiler_params=params(8),
        cost_estimate=cost(0, 8 * rows * width),
        name="join",
    )(place, own, back)


def local(residual, norm_gain, doc_ids, w_query, w_key, w_value, w_out):
    length = doc_ids.shape[0]
    rows, features = residual.shape
    n_z, chip_rows = 4, 2 * rows
    zh, core = lax.axis_index("zh"), lax.axis_index("c")
    column = lax.axis_index("x") * 4 + lax.axis_index("y")
    half = features // 2
    piece = half // 16

    def move(value, by, swap=0):
        perm = [
            (2 * z + c, 2 * ((z + by) % n_z) + (c ^ swap)) for z in range(n_z) for c in range(2)
        ]
        return lax.ppermute(value, ("zh", "c"), perm)

    def swap(value):
        return move(value, 0, 1)

    keep = lax.dynamic_slice_in_dim(w_out, core * half + column * piece, piece, 1)
    give = lax.dynamic_slice_in_dim(w_out, (1 - core) * half + column * piece, piece, 1)
    near = jnp.stack([keep, swap(give)])
    first, second = norm(residual, norm_gain)
    near, first, second = lax.optimization_barrier((near, first, second))
    up_first, down_second = move(first, 1), move(second, -1)
    shifted = [move(near, -r) for r in (1, 2, 3)]
    *shifted, up_first, down_second = lax.optimization_barrier((*shifted, up_first, down_second))
    far = lax.all_gather(jnp.stack(shifted), ("x", "y"), axis=0)

    def relative(values):
        turned = lax.dynamic_slice_in_dim(
            jnp.concatenate([values, values]), zh * chip_rows, length, 0
        ).reshape(n_z, 2, rows)
        return jnp.where(core == 0, turned, turned[:, ::-1]).reshape(n_z, chip_rows)

    documents = relative(doc_ids)
    start = jnp.sum((doc_ids < documents[:, :, None]).astype(jnp.int32), axis=-1)
    chips = (zh + jnp.arange(n_z, dtype=jnp.int32)) % n_z
    cores = core ^ jnp.arange(2, dtype=jnp.int32)
    at = (2 * chips[:, None] + cores)[:, :, None] * rows + jnp.arange(rows, dtype=jnp.int32)
    at = at.reshape(n_z, chip_rows)
    freq = ROPE_BASE ** (-jnp.arange(HD // 2, dtype=F32) / (HD // 2))
    angle = (at - start).astype(F32)[:, :, None] * freq
    cosine, sine = jnp.cos(angle), jnp.sin(angle)
    wide = jnp.broadcast_to(start.astype(F32)[:, :, None], (n_z, chip_rows, HD))
    table = jnp.concatenate([cosine, cosine, -sine, sine, wide, wide], axis=-1)
    place = jnp.concatenate([zh[None], core[None]])

    def heads(blocks, *halves):
        pieces = []
        for a, b in halves:
            pieces += [a, b, swap(a), swap(b)]
        return project(pieces, w_query, w_key, w_value, table, blocks)

    qkv = [None] * 4
    up_second, down_first = move(second, 1), move(first, -1)
    (qkv[0],) = heads((0,), (first, second))
    up_first, down_second, qkv[0] = lax.optimization_barrier((up_first, down_second, qkv[0]))
    far_first, far_second = move(up_first, 1), move(down_second, -1)
    qkv[3], qkv[1], qkv[2] = heads(
        (3, 1, 2), (up_first, up_second), (down_first, down_second), (far_first, far_second)
    )

    own = [None] * 4

    def context(r):
        return attend(r, place, [qkv[r], qkv[(r - 1) % 4], qkv[(r - 2) % 4]], table)

    own[2] = move(context(2), 2)
    sent = context(3)
    own[1] = move(sent, 3)
    sent = context(1)
    own[3] = move(sent, 1)
    qkv[0], own[2] = lax.optimization_barrier((qkv[0], own[2]))
    own[0] = context(0)
    swapped = swap(own[0])

    near_own = lax.dynamic_slice_in_dim(w_out, core * half, half, 1)
    near_other = swap(lax.dynamic_slice_in_dim(w_out, (1 - core) * half, half, 1))
    res_own = lax.dynamic_slice_in_dim(residual, core * half, half, 1)
    res_other = swap(lax.dynamic_slice_in_dim(residual, (1 - core) * half, half, 1))
    total = project_near(own[0], swapped, near_own, near_other)
    own[1], own[3], total = lax.optimization_barrier((own[1], own[3], total))
    other = [swapped] + [swap(part) for part in own[1:]]
    out_own, out_other = project_out(own[1:], other[1:], far, total, res_own, res_other)
    return join(place, out_own, swap(out_other))


def solution(mesh):
    fine = Mesh(mesh.devices.reshape(4, 4, 2, 4, 2), ALL)
    seq, tensor = ("x", "y", "zl"), ("zh", "c")
    placed = (
        P(ALL, None),
        P(),
        P(seq),
        P(None, tensor),
        P(None, tensor),
        P(None, tensor),
        P(tensor, None),
    )
    return jax.shard_map(local, mesh=fine, in_specs=placed, out_specs=P(ALL, None), check_vma=False)
```

```python
import functools
import math

import jax
import jax.numpy as jnp
from jax import lax
from jax.experimental import pallas as pl
from jax.experimental.pallas import tpu as pltpu
from jax.sharding import Mesh, PartitionSpec as P

HD = 128
ROPE_BASE = 500000.0
MIB = 1024 * 1024
F32 = jnp.float32
BF16 = jnp.bfloat16
ALL = ("x", "y", "zl", "zh", "c")


def params(mib):
    return pltpu.CompilerParams(vmem_limit_bytes=mib * MIB)


def cost(flops, bytes_accessed, transcendentals=0):
    return pl.CostEstimate(
        flops=int(flops), bytes_accessed=int(bytes_accessed), transcendentals=int(transcendentals)
    )


def norm_kernel(rows_ref, gain_ref, first_ref, second_ref):
    half = first_ref.shape[0]
    for at, out_ref in ((0, first_ref), (half, second_ref)):
        wide = rows_ref[at : at + half, :].astype(F32)
        scale = lax.rsqrt(jnp.mean(wide * wide, axis=-1, keepdims=True) + 1e-05)
        out_ref[...] = (wide * scale * gain_ref[...]).astype(BF16)


def norm(residual, gain):
    rows, width = residual.shape
    half = jax.ShapeDtypeStruct((rows // 2, width), BF16)
    return pl.pallas_call(
        norm_kernel,
        out_shape=(half, half),
        compiler_params=params(24),
        cost_estimate=cost(4 * rows * width, 4 * rows * width),
        name="norm",
    )(residual, gain.reshape(1, width))


def qkv_kernel(count, *refs):
    pieces, (wq, wk, wv) = refs[:count], refs[count : count + 3]
    groups = count // 4
    tables = refs[count + 3 : count + 3 + groups]
    outs = refs[count + 3 + groups : count + 3 + 2 * groups]
    lhs, weights, lhs_sem, sems = refs[count + 3 + 2 * groups :]
    piece = pieces[0].shape[0]
    rows = 4 * piece
    width = wq.shape[1]
    pair = 2 * HD
    first = [
        pltpu.make_async_copy(part, lhs.at[pl.ds(at * piece, piece), :], lhs_sem.at[at])
        for at, part in enumerate(pieces)
    ]
    loads = [
        [
            pltpu.make_async_copy(wk, weights.at[0, :, pl.ds(0, HD)], sems.at[0]),
            pltpu.make_async_copy(wv, weights.at[0, :, pl.ds(HD, HD)], sems.at[1]),
        ]
    ]
    for at in range(width // pair):
        part = wq.at[:, pl.ds(at * pair, pair)]
        loads.append([pltpu.make_async_copy(part, weights.at[at + 1], sems.at[at + 2])])
    for copy in first + loads[0] + loads[1]:
        copy.start()
    for copy in first:
        copy.wait()
    for step, group in enumerate(loads):
        for copy in group:
            copy.wait()
        if step and step + 1 < len(loads):
            for copy in loads[step + 1]:
                copy.start()
        for block in range(groups):
            table, out_ref = tables[block], outs[block]
            cosine, sine = table[:, :HD], table[:, HD : 2 * HD]

            def turn(part):
                return (part * cosine + pltpu.roll(part, HD // 2, 1) * sine).astype(BF16)

            product = jnp.dot(
                lhs[block * rows : (block + 1) * rows, :],
                weights[step],
                preferred_element_type=F32,
            )
            if step == 0:
                out_ref[:, width : width + HD] = turn(product[:, :HD])
                out_ref[:, width + HD :] = product[:, HD:].astype(BF16)
            else:
                at = (step - 1) * pair
                out_ref[:, at : at + HD] = turn(product[:, :HD])
                out_ref[:, at + HD : at + pair] = turn(product[:, HD:])


def project(pieces, wq, wk, wv, table, blocks):
    piece_rows, depth = pieces[0].shape
    count, groups = len(pieces), len(blocks)
    rows = piece_rows * 4
    width = wq.shape[1] + 2 * HD
    steps = width // (2 * HD)
    anywhere = pl.BlockSpec(memory_space=pl.ANY)

    def angles(at):
        return pl.BlockSpec((None, rows, 2 * HD), lambda k: (at, 0, 0))

    out = jax.ShapeDtypeStruct((rows, width), BF16)
    return pl.pallas_call(
        functools.partial(qkv_kernel, count),
        grid=(1,),
        in_specs=[anywhere] * (count + 3) + [angles(at) for at in blocks],
        out_specs=[pl.BlockSpec((rows, width), lambda k: (0, 0))] * groups,
        out_shape=[out] * groups,
        scratch_shapes=[
            pltpu.VMEM((rows * groups, depth), BF16),
            pltpu.VMEM((steps, depth, 2 * HD), BF16),
            pltpu.SemaphoreType.DMA((count,)),
            pltpu.SemaphoreType.DMA((steps + 1,)),
        ],
        compiler_params=params(58),
        cost_estimate=cost(2 * rows * groups * depth * width, 2 * depth * (rows * groups + width)),
        name="project",
    )(*pieces, wq, wk, wv, *[table] * groups)


def attend_kernel(at, place, q_ref, kv0, kv1, kv2, start_ref, out_ref):
    rows = q_ref.shape[0]
    chip, core = place[0], place[1]

    def index(block, axis):
        local = lax.broadcasted_iota(jnp.int32, (rows, rows), axis)
        local = lax.rem(local + core * (rows // 2), rows)
        return lax.rem(chip + (block % 4), 4) * rows + local

    query_at = index(at, 0)
    start = start_ref[:, :1].astype(jnp.int32)
    bias = []
    for block in (at, at - 1, at - 2):
        key_at = index(block, 1)
        allowed = (key_at <= query_at) & (key_at >= start)
        bias.append(jnp.where(allowed, F32(0.0), F32(-1e30)))
    bias = jnp.concatenate(bias, axis=1)
    keys = jnp.concatenate([kv0[:, :HD], kv1[:, :HD], kv2[:, :HD]], axis=0)
    values = jnp.concatenate([kv0[:, HD:], kv1[:, HD:], kv2[:, HD:]], axis=0)
    tile = rows
    for head in range(0, q_ref.shape[1], HD):
        for row in range(0, rows, tile):
            scores = lax.dot_general(
                q_ref[row : row + tile, head : head + HD],
                keys,
                (((1,), (1,)), ((), ())),
                preferred_element_type=F32,
            )
            scores = scores * F32(math.log2(math.e) / math.sqrt(HD)) + bias[row : row + tile]
            top = jnp.max(scores, axis=-1, keepdims=True)
            expo = jnp.exp2(scores - top)
            total = jnp.sum(expo, axis=-1, keepdims=True)
            context = jnp.dot(expo.astype(BF16), values, preferred_element_type=F32)
            out_ref[row : row + tile, head : head + HD] = (context / total).astype(BF16)


def attend(at, place, blocks, table):
    rows = blocks[0].shape[0]
    width = blocks[0].shape[1] - 2 * HD
    query = pl.BlockSpec((rows, width), lambda h, place: (0, 0))
    pair = pl.BlockSpec((rows, 2 * HD), lambda h, place: (0, width // (2 * HD)))
    return pl.pallas_call(
        functools.partial(attend_kernel, at),
        grid_spec=pltpu.PrefetchScalarGridSpec(
            num_scalar_prefetch=1,
            grid=(1,),
            in_specs=[query]
            + [pair] * 3
            + [pl.BlockSpec((None, rows, HD), lambda h, place: (at, 0, 2))],
            out_specs=query,
        ),
        out_shape=jax.ShapeDtypeStruct((rows, width), BF16),
        compiler_params=params(58),
        cost_estimate=cost(12 * rows * rows * width, 8 * rows * width, 12 * rows * rows),
        name="attend",
    )(place, blocks[0], blocks[0], blocks[1], blocks[2], table)


def times(own, other, low, high):
    half = own.shape[0] // 2
    turned = jnp.concatenate([other[half:, :], other[:half, :]], axis=0)
    total = jnp.dot(own[...], low, preferred_element_type=F32)
    return total + jnp.dot(turned, high, preferred_element_type=F32)


def joined(far, r, e):
    return jnp.concatenate([far[p, r, e] for p in range(far.shape[0])], axis=1)


def near_kernel(own, other, near_own, near_other, total_ref):
    total_ref[...] = times(own, other, near_own[...], near_other[...])


def project_near(own, other, near_own, near_other):
    rows, depth = own.shape
    width, tile = near_own.shape[1], 512
    whole = pl.BlockSpec((rows, depth), lambda n: (0, 0))
    near = pl.BlockSpec((depth, tile), lambda n: (0, n))
    return pl.pallas_call(
        near_kernel,
        grid=(width // tile,),
        in_specs=[whole] * 2 + [near] * 2,
        out_specs=pl.BlockSpec((rows, tile), lambda n: (0, n)),
        out_shape=jax.ShapeDtypeStruct((rows, width), F32),
        compiler_params=params(58),
        cost_estimate=cost(4 * rows * depth * width, 4 * depth * width),
        name="project_near",
    )(own, other, near_own, near_other)


def out_kernel(o1, o2, o3, t1, t2, t3, far, total_ref, res_own, res_other, out_own, out_other):
    half = res_own.shape[0]
    total = total_ref[...]
    for r, (own, other) in enumerate(((o1, t1), (o2, t2), (o3, t3))):
        total = total + times(own, other, joined(far, r, 0), joined(far, r, 1))
    out_own[...] = (res_own[...].astype(F32) + total[:half]).astype(BF16)
    out_other[...] = (res_other[...].astype(F32) + total[half:]).astype(BF16)


def project_out(own, other, far, total, res_own, res_other):
    rows, depth = own[0].shape
    half, width = res_own.shape
    tile, piece = 512, far.shape[-1]
    whole = pl.BlockSpec((rows, depth), lambda n: (0, 0))
    away = pl.BlockSpec((tile // piece, 3, 2, depth, piece), lambda n: (n, 0, 0, 0, 0))
    flat = pl.BlockSpec((half, tile), lambda n: (0, n))
    out = jax.ShapeDtypeStruct((half, width), BF16)
    return pl.pallas_call(
        out_kernel,
        grid=(width // tile,),
        in_specs=[whole] * 6 + [away, pl.BlockSpec((rows, tile), lambda n: (0, n))] + [flat] * 2,
        out_specs=[flat, flat],
        out_shape=[out, out],
        compiler_params=params(58),
        cost_estimate=cost(2 * rows * 6 * depth * width, 12 * depth * width),
        name="project_out",
    )(*own, *other, far, total, res_own, res_other)


def join_kernel(place, own_ref, back_ref, out_ref):
    @pl.when(pl.program_id(0) == 0)
    def _():
        out_ref[...] = own_ref[...]

    @pl.when(pl.program_id(0) == 1)
    def _():
        out_ref[...] = back_ref[...]


def join(place, own, back):
    rows, width = own.shape
    whole = pl.BlockSpec((rows, width), lambda n, place: (0, 0))
    return pl.pallas_call(
        join_kernel,
        grid_spec=pltpu.PrefetchScalarGridSpec(
            num_scalar_prefetch=1,
            grid=(2,),
            in_specs=[whole, whole],
            out_specs=pl.BlockSpec(
                (rows, width), lambda n, place: (0, lax.rem(place[1] + n, 2))
            ),
        ),
        out_shape=jax.ShapeDtypeStruct((rows, 2 * width), BF16),
        compiler_params=params(8),
        cost_estimate=cost(0, 8 * rows * width),
        name="join",
    )(place, own, back)


def local(residual, norm_gain, doc_ids, w_query, w_key, w_value, w_out):
    length = doc_ids.shape[0]
    rows, features = residual.shape
    n_z, chip_rows = 4, 2 * rows
    zh, core = lax.axis_index("zh"), lax.axis_index("c")
    column = lax.axis_index("x") * 4 + lax.axis_index("y")
    half = features // 2
    piece = half // 16

    def move(value, by, swap=0):
        perm = [
            (2 * z + c, 2 * ((z + by) % n_z) + (c ^ swap)) for z in range(n_z) for c in range(2)
        ]
        return lax.ppermute(value, ("zh", "c"), perm)

    def swap(value):
        return move(value, 0, 1)

    keep = lax.dynamic_slice_in_dim(w_out, core * half + column * piece, piece, 1)
    give = lax.dynamic_slice_in_dim(w_out, (1 - core) * half + column * piece, piece, 1)
    near = jnp.stack([keep, swap(give)])
    first, second = norm(residual, norm_gain)
    near, first, second = lax.optimization_barrier((near, first, second))
    up_first, down_second = move(first, 1), move(second, -1)
    shifted = [move(near, -r) for r in (1, 2, 3)]
    *shifted, up_first, down_second = lax.optimization_barrier((*shifted, up_first, down_second))
    far = lax.all_gather(jnp.stack(shifted), ("x", "y"), axis=0)

    def relative(values):
        turned = lax.dynamic_slice_in_dim(
            jnp.concatenate([values, values]), zh * chip_rows, length, 0
        ).reshape(n_z, 2, rows)
        return jnp.where(core == 0, turned, turned[:, ::-1]).reshape(n_z, chip_rows)

    documents = relative(doc_ids)
    start = jnp.sum((doc_ids < documents[:, :, None]).astype(jnp.int32), axis=-1)
    chips = (zh + jnp.arange(n_z, dtype=jnp.int32)) % n_z
    cores = core ^ jnp.arange(2, dtype=jnp.int32)
    at = (2 * chips[:, None] + cores)[:, :, None] * rows + jnp.arange(rows, dtype=jnp.int32)
    at = at.reshape(n_z, chip_rows)
    freq = ROPE_BASE ** (-jnp.arange(HD // 2, dtype=F32) / (HD // 2))
    angle = (at - start).astype(F32)[:, :, None] * freq
    cosine, sine = jnp.cos(angle), jnp.sin(angle)
    wide = jnp.broadcast_to(start.astype(F32)[:, :, None], (n_z, chip_rows, HD))
    table = jnp.concatenate([cosine, cosine, -sine, sine, wide], axis=-1)
    place = jnp.concatenate([zh[None], core[None]])

    def heads(blocks, *halves):
        pieces = []
        for a, b in halves:
            pieces += [a, b, swap(a), swap(b)]
        return project(pieces, w_query, w_key, w_value, table, blocks)

    qkv = [None] * 4
    up_second, down_first = move(second, 1), move(first, -1)
    (qkv[0],) = heads((0,), (first, second))
    up_first, down_second, qkv[0] = lax.optimization_barrier((up_first, down_second, qkv[0]))
    far_first, far_second = move(up_first, 1), move(down_second, -1)
    qkv[3], qkv[1], qkv[2] = heads(
        (3, 1, 2), (up_first, up_second), (down_first, down_second), (far_first, far_second)
    )

    own = [None] * 4

    def context(r):
        return attend(r, place, [qkv[r], qkv[(r - 1) % 4], qkv[(r - 2) % 4]], table)

    own[2] = move(context(2), 2)
    sent = context(3)
    own[1] = move(sent, 3)
    sent = context(1)
    own[3] = move(sent, 1)
    qkv[0], own[2] = lax.optimization_barrier((qkv[0], own[2]))
    own[0] = context(0)
    swapped = swap(own[0])

    near_own = lax.dynamic_slice_in_dim(w_out, core * half, half, 1)
    near_other = swap(lax.dynamic_slice_in_dim(w_out, (1 - core) * half, half, 1))
    res_own = lax.dynamic_slice_in_dim(residual, core * half, half, 1)
    res_other = swap(lax.dynamic_slice_in_dim(residual, (1 - core) * half, half, 1))
    total = project_near(own[0], swapped, near_own, near_other)
    own[1], own[3], total = lax.optimization_barrier((own[1], own[3], total))
    other = [swapped] + [swap(part) for part in own[1:]]
    out_own, out_other = project_out(own[1:], other[1:], far, total, res_own, res_other)
    return join(place, out_own, swap(out_other))


def solution(mesh):
    fine = Mesh(mesh.devices.reshape(4, 4, 2, 4, 2), ALL)
    seq, tensor = ("x", "y", "zl"), ("zh", "c")
    placed = (
        P(ALL, None),
        P(),
        P(seq),
        P(None, tensor),
        P(None, tensor),
        P(None, tensor),
        P(tensor, None),
    )
    return jax.shard_map(local, mesh=fine, in_specs=placed, out_specs=P(ALL, None), check_vma=False)
```
